32 devices in a mesh: gz: 4 (over z), xy: 8 (over y, x, core).
Axes of the slice: x: 2, y: 2, z: 4, core: 2. Of those that a mesh axis runs over, the one named last changes fastest.
Arguments:
- source_inner: float32 [8, 2, 16, 4096], P('gz', None, None, 'xy'), may hold values from -6 to 6
- source_front: float32 [8, 2, 16, 4096], P('gz', None, None, 'xy'), may hold values from -6 to 6
- inner_inverse: bfloat16 [8, 8, 2, 512, 512], P('gz', 'xy'), may hold values from -0.1875 to 0.1875
- coupling: bfloat16 [8, 8, 2, 512, 256], P('gz', 'xy'), may hold values from -0.1875 to 0.1875
- schur_inverse: bfloat16 [8, 2, 4096, 4096], P('gz', None, None, 'xy'), may hold values from -0.046875 to 0.046875
- front_rows: int32 [8, 2048], P('gz', 'xy'), may hold values from 0 to 4095, as said below
- link: float32 [8, 4096], P('gz', 'xy'), may hold values from 0.5 to 1.5
- front_size: int32 [8], P('gz'), may hold values from 2048 to 4096, as said below
Outputs:
- inner_field: float32 [8, 2, 16, 4096], P('gz', None, None, 'xy')
- front_field: float32 [8, 2, 16, 4096], P('gz', None, None, 'xy')
The draws below stay inside these ranges and needn't reach their ends.
Inputs may be any that keep to these rules, and one draw needn't show every extreme that they name: `front_rows`: within one local front of one panel the 256 entries are distinct. `front_size`: some panel has exactly 4096 live unknowns and some exactly half of 4096.
All inputs are finite; a program needn't handle non-finite values.
Results may differ from the reference program's by a relative error of at most 0.0075.
Values may be sent and summed in bfloat16 or wider, within the bound.
No kernel may reach another device: no remote copies, remote signals or barrier semaphores. Data moves between devices by JAX's collectives and lax.ppermute only.
A program may use at most 64 MiB of HBM per device.

```python
import math
import jax
import jax.numpy as jnp
from jax import lax

F = 4096
BND = 256
LOC = 512
RHS = 16
PANELS = 8
N_XY = 8


def draw_front_rows(key, part):
    subkeys = jax.random.split(key, PANELS * N_XY)

    def pick_rows(subkey):
        return jax.random.permutation(subkey, F)[:BND]
    chosen = jax.vmap(pick_rows)(subkeys)
    return chosen.reshape(PANELS, N_XY * BND).astype(jnp.int32)


def draw_front_size(key, part):
    size_key = jax.random.fold_in(key, 11)
    place_key = jax.random.fold_in(key, 12)
    front_sizes = F // 2 + jax.random.randint(size_key, (PANELS,), 0, F // 2 + 1)
    placing = jax.random.permutation(place_key, PANELS)
    front_sizes = front_sizes.at[placing[0]].set(F).at[placing[1]].set(F // 2)
    return front_sizes.astype(jnp.int32)


def steps_of(own_key, extent, pieces, smallest, largest):
    def one(dim, parts):
        heights = jax.random.uniform(jax.random.fold_in(jax.random.fold_in(own_key, 6), dim), (parts,), jnp.float32, smallest / len(pieces), largest / len(pieces))
        return jnp.repeat(jnp.exp(heights), extent[dim] // parts).reshape((-1,) + (1,) * (len(extent) - dim - 1))

    level = one(*pieces[0])
    for cut in pieces[1:]:
        level = level * one(*cut)
    return level


def gaussian(key, extent, width, reach, pieces=(), kind=jnp.bfloat16):
    level = steps_of(key, extent, pieces, -0.22, 0.18) if pieces else 1.0
    drawn = jax.random.normal(key, extent, jnp.float32) * width * level
    return jnp.minimum(jnp.maximum(drawn, -reach), reach).astype(kind)


def setup_inputs(seed: int = 0) -> dict:
    seeds = jax.random.split(jax.random.key(seed), 9)
    source_inner = gaussian(seeds[0], (PANELS, 2, RHS, N_XY * LOC), 1.0, 6.0, ((0, 4), (3, 8)), jnp.float32)
    source_front = gaussian(seeds[1], (PANELS, 2, RHS, F), 1.0, 6.0, ((0, 4), (3, 8)), jnp.float32)
    inner_inverse = gaussian(seeds[2], (PANELS, N_XY, 2, LOC, LOC), (2 * LOC) ** -0.5, 0.1875, ((0, 4), (1, 8)))
    coupling = gaussian(seeds[3], (PANELS, N_XY, 2, LOC, BND), (2 * LOC) ** -0.5, 0.1875, ((0, 4), (1, 8)))
    schur_inverse = gaussian(seeds[4], (PANELS, 2, F, F), (4 * F) ** -0.5, 0.046875, ((0, 4), (3, 8)))
    front_rows = draw_front_rows(jax.random.fold_in(seeds[8], 71), 0)
    link = jnp.clip(jnp.exp(math.log(1.5) - 1.0986123 * jax.random.uniform(seeds[6], (PANELS, F), jnp.float32) ** steps_of(seeds[6], (PANELS, F), ((0, 4), (1, 8)), -0.2, 0.2)), 0.5, 1.5)
    front_size = draw_front_size(jax.random.fold_in(seeds[8], 71), 0)
    return {"source_inner": source_inner, "source_front": source_front, "inner_inverse": inner_inverse, "coupling": coupling, "schur_inverse": schur_inverse, "front_rows": front_rows, "link": link, "front_size": front_size}


def complex_product(field, matrix):
    row_count = field.shape[1]
    flattened = field.astype(jnp.bfloat16).reshape(2 * row_count, field.shape[2])
    first_part = jnp.dot(flattened, matrix[0], preferred_element_type=jnp.float32)
    second = jnp.dot(flattened, matrix[1], preferred_element_type=jnp.float32)
    return jnp.stack([first_part[:row_count] - second[row_count:], second[:row_count] + first_part[row_count:]])


def complex_product_t(field, matrix):
    row_count = field.shape[1]
    flattened = field.astype(jnp.bfloat16).reshape(2 * row_count, field.shape[2])
    contract = (((1,), (1,)), ((), ()))
    first_part = lax.dot_general(flattened, matrix[0], contract, preferred_element_type=jnp.float32)
    second = lax.dot_general(flattened, matrix[1], contract, preferred_element_type=jnp.float32)
    return jnp.stack([first_part[:row_count] - second[row_count:], second[:row_count] + first_part[row_count:]])


def reference(source_inner, source_front, inner_inverse, coupling, schur_inverse, front_rows, link, front_size):
    all_rows = jnp.arange(F, dtype=jnp.int32)
    solved_all = []
    bases = []
    masks = []
    for panel_index in range(PANELS):
        blocks = source_inner[panel_index].reshape(2, RHS, N_XY, LOC).transpose(2, 0, 1, 3)
        solved = jax.vmap(complex_product)(blocks, inner_inverse[panel_index])
        pushed = jax.vmap(complex_product)(solved, coupling[panel_index])
        flat_push = pushed.transpose(1, 2, 0, 3).reshape(2, RHS, N_XY * BND)
        contrib = jnp.zeros((2, RHS, F), jnp.float32).at[:, :, front_rows[panel_index]].add(flat_push)
        solved_all.append(solved)
        bases.append(source_front[panel_index] - contrib)
        masks.append((all_rows < front_size[panel_index]).astype(jnp.float32))
    fronts = []
    incoming = jnp.zeros((2, RHS, F), jnp.float32)
    for panel_index in range(PANELS):
        rhs_front = masks[panel_index] * (bases[panel_index] + link[panel_index] * incoming)
        incoming = masks[panel_index] * complex_product(rhs_front, schur_inverse[panel_index])
        fronts.append(incoming)
    totals = [None] * PANELS
    incoming = jnp.zeros((2, RHS, F), jnp.float32)
    for panel_index in reversed(range(PANELS)):
        change = masks[panel_index] * complex_product(masks[panel_index] * incoming, schur_inverse[panel_index])
        totals[panel_index] = fronts[panel_index] + change
        incoming = link[panel_index] * totals[panel_index]
    inner_out = []
    for panel_index in range(PANELS):
        picked = jnp.take(totals[panel_index], front_rows[panel_index].reshape(N_XY, BND), axis=2)
        picked = picked.transpose(2, 0, 1, 3)
        lifted = jax.vmap(complex_product_t)(picked, coupling[panel_index])
        back_part = jax.vmap(complex_product)(lifted, inner_inverse[panel_index])
        inner = solved_all[panel_index] - back_part
        inner_out.append(inner.transpose(1, 2, 0, 3).reshape(2, RHS, N_XY * LOC))
    return jnp.stack(inner_out), jnp.stack(totals)
```

```python
import functools

import jax
import jax.numpy as jnp
from jax import lax
from jax.experimental import pallas as pl
from jax.experimental.pallas import tpu as pltpu
from jax.sharding import PartitionSpec as P

IN_VMEM = pl.BlockSpec(memory_space=pltpu.VMEM)


def resident(array):
    return pltpu.with_memory_space_constraint(array, pltpu.VMEM)


def complex_product(field, matrix):
    row_count = field.shape[1]
    flattened = field.astype(jnp.bfloat16).reshape(2 * row_count, field.shape[2])
    first_part = jnp.dot(flattened, matrix[0], preferred_element_type=jnp.float32)
    second = jnp.dot(flattened, matrix[1], preferred_element_type=jnp.float32)
    return jnp.stack(
        [first_part[:row_count] - second[row_count:], second[:row_count] + first_part[row_count:]]
    )


def complex_product_t(field, matrix):
    row_count = field.shape[1]
    flattened = field.astype(jnp.bfloat16).reshape(2 * row_count, field.shape[2])
    contract = (((1,), (1,)), ((), ()))
    first_part = lax.dot_general(flattened, matrix[0], contract, preferred_element_type=jnp.float32)
    second = lax.dot_general(flattened, matrix[1], contract, preferred_element_type=jnp.float32)
    return jnp.stack(
        [first_part[:row_count] - second[row_count:], second[:row_count] + first_part[row_count:]]
    )


def swapped(shard, mask):
    peers = lax.axis_size("xy")
    return lax.ppermute(shard, "xy", [(i, i ^ mask) for i in range(peers)])


def gathered_within(message):
    peers = lax.axis_size("xy")
    mine = jnp.stack([message] + [swapped(message, mask) for mask in range(2, peers, 2)])
    return mine, swapped(mine, 1)


def sources_within(peers):
    def sources(me):
        mine = [me ^ mask for mask in range(0, peers, 2)]
        return mine, [peer ^ 1 for peer in mine]

    return sources


def crossed(message, by, keep_mask):
    peers, groups = lax.axis_size("xy"), lax.axis_size("gz")
    half = peers // 4
    pair = jnp.stack([message, swapped(message, 1)])
    parts = []
    for turn in range(half):
        pairs = []
        for group in range(groups):
            for peer in range(peers):
                target = peer ^ (2 * (turn + (peer % 2) * half))
                pairs.append((group * peers + peer, (group + by) % groups * peers + target))
        parts.append(lax.ppermute(pair, ("gz", "xy"), pairs))
    mine = jnp.concatenate(parts)
    if keep_mask is not None:
        mine = jnp.where(keep_mask, mine, jnp.zeros_like(mine))
    return mine, swapped(mine, 1)


def sources_crossed(peers):
    half = peers // 4

    def half_of(me):
        return [
            (me ^ (2 * turn) ^ (me % 2 * (2 * half))) ^ core
            for turn in range(half)
            for core in range(2)
        ]

    def sources(me):
        return half_of(me), half_of(me ^ 1)

    return sources


def step_kernel(panel, turn, sources, has_addend, keeps, *refs):
    mine_ref, other_ref, schur_ref, mask_ref, link_ref = refs[:5]
    addend_ref = refs[5] if has_addend else None
    kept_in, kept_ref, message_ref = refs[-4], refs[-2], refs[-1]

    @pl.when(lax.axis_index("gz") == turn)
    def _():
        row_count, share = mine_ref.shape[2], mine_ref.shape[3]
        mine_from, other_from = sources(lax.axis_index("xy"))
        first = jnp.zeros((2 * row_count, share), jnp.float32)
        second = jnp.zeros((2 * row_count, share), jnp.float32)
        for ref, origins in ((mine_ref, mine_from), (other_ref, other_from)):
            for place, origin in enumerate(origins):
                rows = pl.ds(pl.multiple_of(origin * share, share), share)
                field = ref[place].reshape(2 * row_count, share)
                first += jnp.dot(
                    field, schur_ref[panel, 0, rows, :], preferred_element_type=jnp.float32
                )
                second += jnp.dot(
                    field, schur_ref[panel, 1, rows, :], preferred_element_type=jnp.float32
                )
        mask = mask_ref[...]
        link = link_ref[...]
        values = (
            mask * (first[:row_count] - second[row_count:]),
            mask * (second[:row_count] + first[row_count:]),
        )
        for part, value in enumerate(values):
            if keeps:
                value = kept_in[part] + value
            kept_ref[part] = value
            outgoing = link * value
            if has_addend:
                outgoing = addend_ref[part] + outgoing
            message_ref[part] = outgoing.astype(jnp.bfloat16)


def sweep_step(panel, turn, sources, pieces, schur, mask, link, addend, kept, message, keeps):
    operands = [resident(pieces[0]), resident(pieces[1]), schur, mask, link]
    if addend is not None:
        operands.append(addend)
    count = len(operands)
    return pl.pallas_call(
        functools.partial(step_kernel, panel, turn, sources, addend is not None, keeps),
        out_shape=(
            pltpu.VMEM(kept.shape, kept.dtype),
            pltpu.VMEM(message.shape, message.dtype),
        ),
        in_specs=[IN_VMEM] * (count + 2),
        out_specs=(IN_VMEM, IN_VMEM),
        input_output_aliases={count: 0, count + 1: 1},
        compiler_params=pltpu.CompilerParams(vmem_limit_bytes=40 * 2**20),
    )(*operands, resident(kept), resident(message))


def on_device(
    source_inner, source_front, inner_inverse, coupling, schur_inverse, front_rows, link, front_size
):
    peers, groups = lax.axis_size("xy"), lax.axis_size("gz")
    me = lax.axis_index("xy")
    panel_count, _, side_count, share = source_front.shape
    bound = front_rows.shape[1]
    half = peers // 4
    schur = resident(schur_inverse)
    own_rows = me * share + jnp.arange(share, dtype=jnp.int32)
    masks = [
        (own_rows < front_size[panel]).astype(jnp.float32)[None, :] for panel in range(panel_count)
    ]
    links = [link[panel][None, :] for panel in range(panel_count)]

    solved = [
        complex_product(source_inner[panel], inner_inverse[panel, 0])
        for panel in range(panel_count)
    ]
    pushed = [
        complex_product(solved[panel], coupling[panel, 0]).reshape(2 * side_count, bound)
        for panel in range(panel_count)
    ]
    sent = jnp.concatenate(pushed + [front_rows.astype(jnp.float32)])
    sent = jnp.pad(sent, ((0, -sent.shape[0] % 8), (0, 0)))
    received = lax.all_gather(sent, "xy", axis=1, tiled=True)
    bases = []
    for panel in range(panel_count):
        values = received[2 * side_count * panel : 2 * side_count * (panel + 1)]
        positions = received[2 * side_count * panel_count + panel].astype(jnp.int32)
        hits = (positions[:, None] == own_rows[None, :]).astype(jnp.bfloat16)
        high = values.astype(jnp.bfloat16)
        low = (values - high.astype(jnp.float32)).astype(jnp.bfloat16)
        summed = jnp.dot(jnp.concatenate([high, low]), hits, preferred_element_type=jnp.float32)
        summed = summed[: 2 * side_count] + summed[2 * side_count :]
        contrib = summed.reshape(2, side_count, share)
        bases.append(masks[panel] * (source_front[panel] - contrib))

    forward_links = [masks[panel] * links[panel] for panel in range(panel_count)]
    packed = jnp.concatenate(
        [bases[0].reshape(2 * side_count, share), jnp.tile(forward_links[0], (8, 1))]
    )
    packed = lax.ppermute(packed, "gz", [(g, (g - 1) % groups) for g in range(groups)])
    next_base = packed[: 2 * side_count].reshape(2, side_count, share)
    next_link = packed[2 * side_count : 2 * side_count + 1]
    backward_links = [
        links[panel] * masks[panel - 1] if panel else links[0] for panel in range(panel_count)
    ]
    own_masks = [resident(mask) for mask in masks]
    forward_addends = [resident(base) for base in bases[1:] + [next_base]]
    forward_scales = [resident(scale) for scale in forward_links[1:] + [next_link]]
    backward_scales = [resident(scale) for scale in backward_links]
    arriving = jnp.stack(sources_crossed(peers)(me)[0]).reshape(2 * half, 1, 1, 1)
    arriving_rows = arriving * share + jnp.arange(share, dtype=jnp.int32)
    arriving_mask = arriving_rows < front_size[panel_count - 1]

    kept = [jnp.zeros((2, side_count, share), jnp.float32) for _ in range(panel_count)]
    message = bases[0].astype(jnp.bfloat16)
    within, across = sources_within(peers), sources_crossed(peers)
    pieces, sources = gathered_within(message), within
    for turn in range(groups):
        for panel in range(panel_count):
            last = turn == groups - 1 and panel == panel_count - 1
            kept[panel], message = sweep_step(
                panel, turn, sources, pieces, schur, own_masks[panel],
                backward_scales[panel] if last else forward_scales[panel],
                None if last else forward_addends[panel],
                kept[panel], message, False,
            )
            if panel < panel_count - 1 or last:
                pieces, sources = gathered_within(message), within
            else:
                pieces, sources = crossed(message, 1, None), across
    if panel_count == 1 and groups > 1:
        pieces, sources = crossed(message, -1, arriving_mask), across
    for turn in reversed(range(groups)):
        for panel in reversed(range(panel_count)):
            if turn == groups - 1 and panel == panel_count - 1:
                continue
            kept[panel], message = sweep_step(
                panel, turn, sources, pieces, schur, own_masks[panel],
                backward_scales[panel], None, kept[panel], message, True,
            )
            if panel > 0:
                pieces, sources = gathered_within(message), within
            elif turn > 0:
                pieces, sources = crossed(message, -1, arriving_mask), across

    fronts = jnp.stack(kept)
    everywhere = lax.all_gather(fronts.astype(jnp.bfloat16), "xy", axis=3, tiled=True)
    all_rows = jnp.arange(everywhere.shape[3], dtype=jnp.int32)
    inner_out = []
    for panel in range(panel_count):
        chosen = (all_rows[:, None] == front_rows[panel][None, :]).astype(jnp.bfloat16)
        flat = everywhere[panel].reshape(2 * side_count, everywhere.shape[3])
        picked = jnp.dot(flat, chosen, preferred_element_type=jnp.float32)
        picked = picked.reshape(2, side_count, bound)
        lifted = complex_product_t(picked, coupling[panel, 0])
        inner_out.append(solved[panel] - complex_product(lifted, inner_inverse[panel, 0]))
    return (jnp.stack(inner_out), fronts)


def solution(mesh):
    placed = (
        P("gz", None, None, "xy"),
        P("gz", None, None, "xy"),
        P("gz", "xy", None, None, None),
        P("gz", "xy", None, None, None),
        P("gz", None, None, "xy"),
        P("gz", "xy"),
        P("gz", "xy"),
        P("gz"),
    )
    return jax.shard_map(
        on_device,
        mesh=mesh,
        in_specs=placed,
        out_specs=(P("gz", None, None, "xy"), P("gz", None, None, "xy")),
        check_vma=False,
    )
```

```python
import functools

import jax
import jax.numpy as jnp
from jax import lax
from jax.experimental import pallas as pl
from jax.experimental.pallas import tpu as pltpu
from jax.sharding import PartitionSpec as P

IN_VMEM = pl.BlockSpec(memory_space=pltpu.VMEM)


IN_HBM = pl.BlockSpec(memory_space=pltpu.HBM)
IN_SMEM = pl.BlockSpec(memory_space=pltpu.SMEM)


def resident(array):
    return pltpu.with_memory_space_constraint(array, pltpu.VMEM)


def in_hbm(array):
    return pltpu.with_memory_space_constraint(array, pltpu.HBM)


def swapped(shard, mask):
    peers = lax.axis_size("xy")
    return lax.ppermute(shard, "xy", [(i, i ^ mask) for i in range(peers)])


def gathered_within(message, beside=None):
    peers = lax.axis_size("xy")
    fetched = [swapped(message, mask) for mask in reversed(range(2, peers, 2))]
    if beside is not None:
        fetched, beside = lax.optimization_barrier((fetched, beside))
    mine = jnp.stack([message] + fetched[::-1])
    pieces = mine, swapped(mine, 1)
    return pieces if beside is None else (pieces, beside)


def sources_within(peers):
    def sources(me):
        mine = [me ^ mask for mask in range(0, peers, 2)]
        return mine, [peer ^ 1 for peer in mine]

    return sources


def crossed(message, by, arrive):
    peers, groups = lax.axis_size("xy"), lax.axis_size("gz")
    half = peers // 4
    pair = jnp.stack([message, swapped(message, 1)])
    parts = []
    for turn in range(half):
        pairs = []
        for group in range(groups):
            for peer in range(peers):
                target = peer ^ (2 * (turn + (peer % 2) * half))
                pairs.append((group * peers + peer, (group + by) % groups * peers + target))
        parts.append(lax.ppermute(pair, ("gz", "xy"), pairs))
    mine = arrive(jnp.concatenate(parts))
    return mine, swapped(mine, 1)


def sources_crossed(peers):
    half = peers // 4

    def half_of(me):
        return [
            (me ^ (2 * turn) ^ (me % 2 * (2 * half))) ^ core
            for turn in range(half)
            for core in range(2)
        ]

    def sources(me):
        return half_of(me), half_of(me ^ 1)

    return sources


def gated(turn):
    def wrap(body):
        if turn is None:
            body()
        else:
            pl.when(lax.axis_index("gz") == turn)(body)

    return wrap


def in_kernel(body, outs, operands, aliases=None, specs=None, scratch=(), flops=0, moved=0):
    return pl.pallas_call(
        body,
        out_shape=tuple(pltpu.VMEM(shape, dtype) for shape, dtype in outs),
        in_specs=specs or [IN_VMEM] * len(operands),
        out_specs=(IN_VMEM,) * len(outs),
        scratch_shapes=scratch,
        input_output_aliases=aliases or {},
        compiler_params=pltpu.CompilerParams(vmem_limit_bytes=16 * 2**20),
        cost_estimate=pl.CostEstimate(flops=flops, bytes_accessed=moved, transcendentals=0),
    )(*operands)


def real_products(field, matrix):
    return [
        jnp.dot(field, matrix[part], preferred_element_type=jnp.float32) for part in range(2)
    ]


def combined(products):
    first, second = products
    count = first.shape[0] // 2
    return first[:count] - second[count:], second[:count] + first[count:]


def load_kernel(panel, chunks, schur_ref, after_ref, out_ref, sems):
    del after_ref
    rows = schur_ref.shape[2] // chunks
    copies = []
    for part in range(2):
        for chunk in range(chunks):
            span = pl.ds(chunk * rows, rows)
            copies.append(
                pltpu.make_async_copy(
                    schur_ref.at[panel, part, span, :],
                    out_ref.at[part, span, :],
                    sems.at[part * chunks + chunk],
                )
            )
    for copy in copies:
        copy.start()
    for copy in copies:
        copy.wait()


def loaded(panel, schur, after):
    chunks = 4
    shape = schur.shape[1:]
    return in_kernel(
        functools.partial(load_kernel, panel, chunks),
        [(shape, schur.dtype)],
        [in_hbm(schur), after],
        specs=[IN_HBM, pl.BlockSpec(memory_space=pl.ANY)],
        scratch=[pltpu.SemaphoreType.DMA((2 * chunks,))],
        moved=2 * schur.dtype.itemsize * shape[0] * shape[1] * shape[2],
    )[0]


def local_kernel(*refs):
    operands, (solved_ref, sent_ref), held, sems = refs[:6], refs[6:8], refs[8:14], refs[14]
    source_ref, inverse_ref, coupling_ref, rows_ref, link_ref, _ = held
    panel_count, _, side_count, _ = source_ref.shape
    copies = [
        pltpu.make_async_copy(operand, place, sems.at[index])
        for index, (operand, place) in enumerate(zip(operands, held))
    ]
    for copy in copies:
        copy.start()
    copies[0].wait()
    copies[1].wait()
    fields = []
    for panel in range(panel_count):
        field = source_ref[panel].astype(jnp.bfloat16).reshape(2 * side_count, -1)
        solved = combined(real_products(field, inverse_ref.at[panel, 0]))
        for part in range(2):
            solved_ref[panel, part] = solved[part]
        fields.append(jnp.concatenate(solved).astype(jnp.bfloat16))
    copies[2].wait()
    row = 0
    for panel in range(panel_count):
        pushed = combined(real_products(fields[panel], coupling_ref.at[panel, 0]))
        for part in range(2):
            sent_ref[pl.ds(row, side_count), :] = pushed[part]
            row += side_count
    for copy in copies[3:]:
        copy.wait()
    bound = sent_ref.shape[1]
    sent_ref[pl.ds(row, sent_ref.shape[0] - row), :] = jnp.zeros(
        (sent_ref.shape[0] - row, bound), jnp.float32
    )
    sent_ref[pl.ds(row, panel_count), :] = rows_ref[...].astype(jnp.float32)
    row += panel_count
    share = link_ref.shape[1]
    for start in range(0, share, bound):
        width = min(bound, share - start)
        sent_ref[pl.ds(row, 1), pl.ds(0, width)] = link_ref[pl.ds(0, 1), pl.ds(start, width)]
        row += 1


def live(size_ref, panel, start, share):
    rows = start + lax.broadcasted_iota(jnp.int32, (1, share), 1)
    return jnp.where(rows < size_ref[panel], 1.0, 0.0)


def base_kernel(panel, panel_count, size_ref, mine_ref, other_ref, source_ref, base_ref, message_ref):
    _, side_count, share = base_ref.shape
    bound = mine_ref.shape[2]
    count = 2 * side_count
    start = lax.axis_index("xy") * share
    own_rows = start + lax.broadcasted_iota(jnp.int32, (share, bound), 0)
    contract = (((1,), (1,)), ((), ()))
    total = jnp.zeros((2 * count, share), jnp.float32)
    for ref in (mine_ref, other_ref):
        for place in range(ref.shape[0]):
            values = ref[place, pl.ds(count * panel, count), :]
            places = ref[place, pl.ds(count * panel_count + panel, 1), :].astype(jnp.int32)
            hits = jnp.where(own_rows == places, 1.0, 0.0).astype(jnp.bfloat16)
            high = values.astype(jnp.bfloat16)
            low = (values - high.astype(jnp.float32)).astype(jnp.bfloat16)
            total += lax.dot_general(
                jnp.concatenate([high, low]), hits, contract, preferred_element_type=jnp.float32
            )
    contrib = total[:count] + total[count:]
    mask = live(size_ref, panel, start, share)
    for part in range(2):
        rows = slice(part * side_count, (part + 1) * side_count)
        base = mask * (source_ref[panel, part] - contrib[rows])
        base_ref[part] = base
        message_ref[part] = base.astype(jnp.bfloat16)


def scales_kernel(panel_count, side_count, size_ref, link_ref, mine_ref, other_ref, *outs):
    share, bound = link_ref.shape[1], mine_ref.shape[2]
    me = lax.axis_index("xy")
    half = mine_ref.shape[0] // 2
    masks = [live(size_ref, panel, me * share, share) for panel in range(panel_count)]
    for panel in range(panel_count):
        link = link_ref[pl.ds(panel, 1), :]
        outs[panel][...] = masks[panel]
        outs[panel_count + panel][...] = masks[panel] * link
        outs[2 * panel_count + panel][...] = link * masks[panel - 1] if panel else link
    forward_ref, backward_ref = outs[3 * panel_count :]
    first = panel_count * (2 * side_count + 1)
    origins = sources_crossed(4 * half)(me)[0]
    for index, origin in enumerate(origins):
        ref = (mine_ref, other_ref)[index % 2]
        place = index // 2 + me % 2 * half
        reached = live(size_ref, 0, origin * share, share)
        backward_ref[index, 0] = live(size_ref, panel_count - 1, origin * share, share)
        for piece, start in enumerate(range(0, share, bound)):
            width = min(bound, share - start)
            link = ref[place, pl.ds(first + piece, 1), pl.ds(0, width)]
            forward_ref[index, 0, :, pl.ds(start, width)] = reached[:, start : start + width] * link


def part_products(ref, origins, schur_ref, products):
    side_count, share = ref.shape[2:]
    for place, origin in enumerate(origins):
        rows = pl.ds(pl.multiple_of(origin * share, share), share)
        field = ref[place].reshape(2 * side_count, share)
        terms = real_products(field, schur_ref.at[:, rows, :])
        products = terms if products is None else [a + b for a, b in zip(products, terms)]
    return products


def early_kernel(turn, sources, mine_ref, schur_ref, products_ref):
    @gated(turn)
    def _():
        origins = sources(lax.axis_index("xy"))[0]
        products = part_products(mine_ref, origins, schur_ref, None)
        for part in range(2):
            products_ref[part] = products[part]


def late_kernel(turn, sources, names, *refs):
    named = dict(zip(names, refs))
    kept_ref, message_ref = refs[-2:]

    @gated(turn)
    def _():
        origins = sources(lax.axis_index("xy"))[1]
        products = [named["products"][part] for part in range(2)]
        products = part_products(named["other"], origins, named["schur"], products)
        for part, value in enumerate(combined(products)):
            value = named["mask"][...] * value
            if "kept" in named:
                value = named["kept"][part] + value
            kept_ref[part] = value
            if "scale" in named:
                value = named["scale"][...] * value
            if "addend" in named:
                value = named["addend"][part] + value
            message_ref[part] = value.astype(jnp.bfloat16)


def sweep_step(turn, sources, pieces, schur, kept, message, **others):
    mine, other = pieces
    shape = kept.shape
    count = 2 * shape[1]
    flops = 4 * count * shape[2] * shape[2] * mine.shape[0]
    moved = 4 * shape[2] * shape[2] * mine.shape[0]
    products = in_kernel(
        functools.partial(early_kernel, turn, sources),
        [((2, count, shape[2]), jnp.float32)],
        [resident(mine), resident(schur)],
        flops=flops,
        moved=moved,
    )[0]
    named = {"products": products, "other": other, "schur": schur}
    named.update({name: value for name, value in others.items() if value is not None})
    named["kept"], named["message"] = kept, message
    names = list(named)
    if others.get("adds", True) is None:
        names[names.index("kept")] = "old"
    operands = [resident(value) for name, value in named.items() if name != "adds"]
    names = [name for name in names if name != "adds"]
    return in_kernel(
        functools.partial(late_kernel, turn, sources, names),
        [(kept.shape, kept.dtype), (message.shape, message.dtype)],
        operands,
        aliases={len(names) - 2: 0, len(names) - 1: 1},
        flops=flops,
        moved=moved,
    )


def pick_kernel(mine_ref, rows_ref, picked_ref):
    picked = picks(mine_ref, rows_ref, sources_within_list(mine_ref.shape[0])[0])
    for panel, value in enumerate(picked):
        picked_ref[panel] = value


def sources_within_list(chips):
    return sources_within(2 * chips)(lax.axis_index("xy"))


def picks(ref, rows_ref, origins):
    _, panel_count, _, side_count, share = ref.shape
    bound = rows_ref.shape[1]
    found = []
    for panel in range(panel_count):
        total = jnp.zeros((2 * side_count, bound), jnp.float32)
        for place, origin in enumerate(origins):
            rows = origin * share + lax.broadcasted_iota(jnp.int32, (share, bound), 0)
            chosen = jnp.where(rows == rows_ref[pl.ds(panel, 1), :], 1.0, 0.0).astype(jnp.bfloat16)
            field = ref[place, panel].reshape(2 * side_count, share)
            total += jnp.dot(field, chosen, preferred_element_type=jnp.float32)
        found.append(total)
    return found


def inner_kernel(picked_ref, other_ref, rows_ref, coupling_ref, inverse_ref, solved_ref, out_ref):
    contract = (((1,), (1,)), ((), ()))
    more = picks(other_ref, rows_ref, sources_within_list(other_ref.shape[0])[1])
    for panel, value in enumerate(more):
        picked = (picked_ref[panel] + value).astype(jnp.bfloat16)
        lifted = combined(
            [
                lax.dot_general(
                    picked, coupling_ref[panel, 0, part], contract, preferred_element_type=jnp.float32
                )
                for part in range(2)
            ]
        )
        field = jnp.concatenate(lifted).astype(jnp.bfloat16)
        back = combined(real_products(field, inverse_ref.at[panel, 0]))
        for part in range(2):
            out_ref[panel, part] = solved_ref[panel, part] - back[part]


def on_device(
    source_inner, source_front, inner_inverse, coupling, schur_inverse, front_rows, link, front_size
):
    peers, groups = lax.axis_size("xy"), lax.axis_size("gz")
    panel_count, _, side_count, share = source_front.shape
    bound = front_rows.shape[1]
    half = peers // 4
    local = source_inner.shape[3]

    link_rows = -(-share // bound)
    sent_rows = panel_count * (2 * side_count + 1) + link_rows
    sent_rows += -sent_rows % 8
    taken = [source_inner, inner_inverse, coupling, front_rows, link, source_front]
    solved, sent, _, inverse_held, coupling_held, rows_held, link_held, source_held = in_kernel(
        local_kernel,
        [
            ((panel_count, 2, side_count, local), jnp.float32),
            ((sent_rows, bound), jnp.float32),
        ]
        + [(value.shape, value.dtype) for value in taken],
        [in_hbm(value) for value in taken],
        specs=[IN_HBM] * len(taken),
        scratch=[pltpu.SemaphoreType.DMA((len(taken),))],
    )
    (mine, other), first_schur = gathered_within(sent, loaded(0, schur_inverse, sent))
    schurs = [first_schur]
    mine, other = resident(mine), resident(other)
    bases, messages = [], []
    for panel in range(panel_count):
        base, message = in_kernel(
            functools.partial(base_kernel, panel, panel_count),
            [((2, side_count, share), jnp.float32), ((2, side_count, share), jnp.bfloat16)],
            [front_size, mine, other, resident(source_held)],
            specs=[IN_SMEM] + [IN_VMEM] * 3,
            moved=2**22,
        )
        bases.append(base)
        messages.append(message)

    row = ((1, share), jnp.float32)
    arriving = ((2 * half, 1, 1, share), jnp.float32)
    scales = in_kernel(
        functools.partial(scales_kernel, panel_count, side_count),
        [row] * (3 * panel_count) + [arriving] * 2,
        [front_size, resident(link_held), mine, other],
        specs=[IN_SMEM] + [IN_VMEM] * 3,
    )
    masks, forward_scales = scales[:panel_count], scales[panel_count : 2 * panel_count]
    backward_scales = scales[2 * panel_count : 3 * panel_count]
    arriving_forward, arriving_backward = scales[3 * panel_count :]

    def arrive_forward(pieces):
        return (arriving_forward * pieces.astype(jnp.float32)).astype(jnp.bfloat16)

    def arrive_backward(pieces):
        return (arriving_backward * pieces.astype(jnp.float32)).astype(jnp.bfloat16)

    kept = [jnp.zeros((2, side_count, share), jnp.float32) for _ in range(panel_count)]
    message = messages[0]
    within, across = sources_within(peers), sources_crossed(peers)
    rest = [loaded(panel, schur_inverse, message) for panel in range(1, panel_count)]
    (pieces, rest), sources = gathered_within(message, rest), within
    schurs += rest
    for turn in range(-1, groups):
        for panel in range(panel_count):
            own = turn == -1 and panel == 0
            if (turn == -1 and panel > 0) or (turn == 0 and panel == 0):
                continue
            ends = panel == panel_count - 1
            last = turn == groups - 1 and ends
            scale = addend = None
            if last:
                scale = backward_scales[panel]
            elif not ends:
                scale, addend = forward_scales[panel + 1], bases[panel + 1]
            kept[panel], message = sweep_step(
                None if own else turn, sources, pieces, schurs[panel], kept[panel], message,
                mask=masks[panel], scale=scale, addend=addend,
                adds=True if panel == 0 and not own else None,
            )
            if not ends or last:
                pieces, sources = gathered_within(message), within
            else:
                pieces, sources = crossed(message, 1, arrive_forward), across
    for turn in reversed(range(groups)):
        for panel in reversed(range(panel_count)):
            if turn == groups - 1 and panel == panel_count - 1:
                continue
            kept[panel], message = sweep_step(
                turn, sources, pieces, schurs[panel], kept[panel], message,
                mask=masks[panel], scale=backward_scales[panel], adds=True,
            )
            if panel > 0:
                pieces, sources = gathered_within(message), within
            elif turn > 0:
                pieces, sources = crossed(message, -1, arrive_backward), across

    fronts = jnp.stack(kept)
    mine, other = gathered_within(fronts.astype(jnp.bfloat16))
    picked = in_kernel(
        pick_kernel,
        [((panel_count, 2 * side_count, bound), jnp.float32)],
        [resident(mine), resident(rows_held)],
        moved=2**22,
    )[0]
    inner = in_kernel(
        inner_kernel,
        [(solved.shape, jnp.float32)],
        [
            resident(value)
            for value in (picked, other, rows_held, coupling_held, inverse_held, solved)
        ],
    )[0]
    return inner, fronts


def solution(mesh):
    placed = (
        P("gz", None, None, "xy"),
        P("gz", None, None, "xy"),
        P("gz", "xy", None, None, None),
        P("gz", "xy", None, None, None),
        P("gz", None, None, "xy"),
        P("gz", "xy"),
        P("gz", "xy"),
        P("gz"),
    )
    return jax.shard_map(
        on_device,
        mesh=mesh,
        in_specs=placed,
        out_specs=(P("gz", None, None, "xy"), P("gz", None, None, "xy")),
        check_vma=False,
    )
```

```python
import functools

import jax
import jax.numpy as jnp
from jax import lax
from jax.experimental import pallas as pl
from jax.experimental.pallas import tpu as pltpu
from jax.sharding import PartitionSpec as P

IN_VMEM = pl.BlockSpec(memory_space=pltpu.VMEM)


IN_HBM = pl.BlockSpec(memory_space=pltpu.HBM)
IN_SMEM = pl.BlockSpec(memory_space=pltpu.SMEM)


def resident(array):
    return pltpu.with_memory_space_constraint(array, pltpu.VMEM)


def in_hbm(array):
    return pltpu.with_memory_space_constraint(array, pltpu.HBM)


def swapped(shard, mask):
    peers = lax.axis_size("xy")
    return lax.ppermute(shard, "xy", [(i, i ^ mask) for i in range(peers)])


def masks_within(peers):
    masks = [0] + list(reversed(range(2, peers, 2)))
    return masks[: peers // 4], masks[peers // 4 :]


def in_halves(one, fetched, join, first, beside=()):
    pieces = [(one, swapped(one, 1))]
    made = first(one)
    fetched, made, beside = lax.optimization_barrier((fetched, made, beside))
    two = join(fetched)
    pieces.append((two, swapped(two, 1)))
    return pieces, made, beside


def gathered_within(message, first, beside=()):
    masks = masks_within(lax.axis_size("xy"))
    one, two = [
        [swapped(message, mask) if mask else message for mask in half] for half in masks
    ]
    return in_halves(jnp.stack(one), two, jnp.stack, first, beside)


def sources_within(peers):
    def sources(me):
        found = []
        for masks in masks_within(peers):
            mine = [me ^ mask for mask in masks]
            found.append((mine, [peer ^ 1 for peer in mine]))
        return found

    return sources


def crossed(message, low, arrive, first):
    peers, groups = lax.axis_size("xy"), lax.axis_size("gz")
    half = peers // 4
    pair = jnp.stack([message, swapped(message, 1)])
    parts = []
    for turn in range(half):
        pairs = []
        for group in range(groups):
            for peer in range(peers):
                if group in (low, low + 1):
                    place = (2 * low + 1 - group) * peers + (peer ^ (2 * (turn + peer % 2 * half)))
                else:
                    place = group * peers + (peer ^ 1)
                pairs.append((group * peers + peer, place))
        parts.append(lax.ppermute(pair, ("gz", "xy"), pairs))
    one = arrive(jnp.concatenate(parts[: half // 2]), 0)
    return in_halves(
        one, parts[half // 2 :], lambda rest: arrive(jnp.concatenate(rest), 1), first
    )[:2]


def sources_crossed(peers):
    half = peers // 4

    def half_of(me, turns):
        return [
            (me ^ (2 * turn) ^ (me % 2 * (2 * half))) ^ core for turn in turns for core in range(2)
        ]

    def sources(me):
        return [
            (half_of(me, turns), half_of(me ^ 1, turns))
            for turns in (range(half // 2), range(half // 2, half))
        ]

    return sources


def gated(turn):
    def wrap(body):
        if turn is None:
            body()
        else:
            pl.when(lax.axis_index("gz") == turn)(body)

    return wrap


def in_kernel(body, outs, operands, aliases=None, specs=None, scratch=(), flops=0, moved=0):
    return pl.pallas_call(
        body,
        out_shape=tuple(pltpu.VMEM(shape, dtype) for shape, dtype in outs),
        in_specs=specs or [IN_VMEM] * len(operands),
        out_specs=(IN_VMEM,) * len(outs),
        scratch_shapes=scratch,
        input_output_aliases=aliases or {},
        compiler_params=pltpu.CompilerParams(vmem_limit_bytes=16 * 2**20),
        cost_estimate=pl.CostEstimate(flops=flops, bytes_accessed=moved, transcendentals=0),
    )(*operands)


def real_products(field, matrix):
    return [
        jnp.dot(field, matrix[part], preferred_element_type=jnp.float32) for part in range(2)
    ]


def combined(products):
    first, second = products
    count = first.shape[0] // 2
    return first[:count] - second[count:], second[:count] + first[count:]


def load_kernel(panel, chunks, schur_ref, after_ref, out_ref, sems):
    del after_ref
    rows = schur_ref.shape[2] // chunks
    copies = []
    for part in range(2):
        for chunk in range(chunks):
            span = pl.ds(chunk * rows, rows)
            copies.append(
                pltpu.make_async_copy(
                    schur_ref.at[panel, part, span, :],
                    out_ref.at[part, span, :],
                    sems.at[part * chunks + chunk],
                )
            )
    for copy in copies:
        copy.start()
    for copy in copies:
        copy.wait()


def loaded(panel, schur, after):
    chunks = 4
    shape = schur.shape[1:]
    return in_kernel(
        functools.partial(load_kernel, panel, chunks),
        [(shape, schur.dtype)],
        [in_hbm(schur), after],
        specs=[IN_HBM, pl.BlockSpec(memory_space=pl.ANY)],
        scratch=[pltpu.SemaphoreType.DMA((2 * chunks,))],
        moved=2 * schur.dtype.itemsize * shape[0] * shape[1] * shape[2],
    )[0]


def local_kernel(*refs):
    operands, (solved_ref, sent_ref), held, (tail_ref, sems) = refs[:6], refs[6:8], refs[8:14], refs[14:]
    source_ref, inverse_ref, coupling_ref, rows_ref, link_ref, _ = held
    panel_count, _, side_count, _ = source_ref.shape
    bound, share = sent_ref.shape[1], link_ref.shape[1]
    copies = []
    for index, (operand, place) in enumerate(zip(operands, held)):
        for panel in range(panel_count):
            copies.append(
                pltpu.make_async_copy(
                    operand.at[panel], place.at[panel], sems.at[index * panel_count + panel]
                )
            )
    by_operand = [copies[i * panel_count : (i + 1) * panel_count] for i in range(len(operands))]
    for panel in range(panel_count):
        for index in range(3):
            by_operand[index][panel].start()
    for group in by_operand[3:]:
        for copy in group:
            copy.start()
    for panel in range(panel_count):
        by_operand[0][panel].wait()
        by_operand[1][panel].wait()
        field = source_ref[panel].astype(jnp.bfloat16).reshape(2 * side_count, -1)
        solved = combined(real_products(field, inverse_ref.at[panel, 0]))
        for part in range(2):
            solved_ref[panel, part] = solved[part]
        field = jnp.concatenate(solved).astype(jnp.bfloat16)
        by_operand[2][panel].wait()
        pushed = combined(real_products(field, coupling_ref.at[panel, 0]))
        for part in range(2):
            start = (2 * panel + part) * side_count
            sent_ref[pl.ds(start, side_count), :] = pushed[part].astype(jnp.bfloat16)
    for group in by_operand[3:]:
        for copy in group:
            copy.wait()
    tail_ref[...] = jnp.zeros(tail_ref.shape, jnp.float32)
    for panel in range(panel_count):
        rows = rows_ref[pl.ds(panel, 1), :]
        tail_ref[pl.ds(panel, 1), :] = (rows >> 8).astype(jnp.float32)
        tail_ref[pl.ds(panel_count + panel, 1), :] = (rows & 255).astype(jnp.float32)
    row = 2 * panel_count
    for start in range(0, share, bound):
        width = min(bound, share - start)
        link = link_ref[pl.ds(0, 1), pl.ds(start, width)]
        high = link.astype(jnp.bfloat16).astype(jnp.float32)
        tail_ref[pl.ds(row, 1), pl.ds(0, width)] = high
        tail_ref[pl.ds(row + 1, 1), pl.ds(0, width)] = link - high
        row += 2
    first = 2 * side_count * panel_count
    sent_ref[pl.ds(first, tail_ref.shape[0]), :] = tail_ref[...].astype(jnp.bfloat16)


def tail_of(ref, place, first):
    return ref[place, pl.ds(first, ref.shape[1] - first), :].astype(jnp.float32)


def live(size_ref, panel, start, share):
    rows = start + lax.broadcasted_iota(jnp.int32, (1, share), 1)
    return jnp.where(rows < size_ref[panel], 1.0, 0.0)


def pushed_up(panel, panel_count, count, share, refs, contrib):
    bound = refs[0].shape[2]
    own_rows = lax.axis_index("xy") * share + lax.broadcasted_iota(jnp.int32, (share, bound), 0)
    contract = (((1,), (1,)), ((), ()))
    for ref in refs:
        for place in range(ref.shape[0]):
            values = ref[place, pl.ds(count * panel, count), :]
            tail = tail_of(ref, place, count * panel_count)
            high = tail[panel : panel + 1]
            low = tail[panel_count + panel : panel_count + panel + 1]
            places = (256.0 * high + low).astype(jnp.int32)
            hits = jnp.where(own_rows == places, 1.0, 0.0).astype(jnp.bfloat16)
            contrib += lax.dot_general(values, hits, contract, preferred_element_type=jnp.float32)
    return contrib


def push_kernel(panel, panel_count, *refs):
    refs, contrib_ref = refs[:-1], refs[-1]
    count, share = contrib_ref.shape
    zeros = jnp.zeros((count, share), jnp.float32)
    contrib_ref[...] = pushed_up(panel, panel_count, count, share, refs, zeros)


def base_kernel(panel, panel_count, size_ref, contrib_ref, source_ref, *refs):
    refs, base_ref, message_ref = refs[:-2], refs[-2], refs[-1]
    _, side_count, share = base_ref.shape
    count = 2 * side_count
    contrib = pushed_up(panel, panel_count, count, share, refs, contrib_ref[...])
    mask = live(size_ref, panel, lax.axis_index("xy") * share, share)
    for part in range(2):
        rows = slice(part * side_count, (part + 1) * side_count)
        base = mask * (source_ref[panel, part] - contrib[rows])
        base_ref[part] = base
        message_ref[part] = base.astype(jnp.bfloat16)


def scales_kernel(panel_count, side_count, size_ref, link_ref, *refs):
    shards, outs = refs[:4], refs[4:]
    share, bound = link_ref.shape[1], shards[0].shape[2]
    peers = 2 * (shards[0].shape[0] + shards[2].shape[0])
    me = lax.axis_index("xy")
    masks = [live(size_ref, panel, me * share, share) for panel in range(panel_count)]
    for panel in range(panel_count):
        link = link_ref[pl.ds(panel, 1), :]
        outs[panel][...] = masks[panel]
        outs[panel_count + panel][...] = masks[panel] * link
        outs[2 * panel_count + panel][...] = link * masks[panel - 1] if panel else link
    arriving = outs[3 * panel_count :]
    first = 2 * side_count * panel_count
    links = {}
    for half, masks_half in enumerate(masks_within(peers)):
        for core in range(2):
            for place, mask in enumerate(masks_half):
                tail = tail_of(shards[2 * half + core], place, first)
                found = []
                for piece, start in enumerate(range(0, share, bound)):
                    row = 2 * (panel_count + piece)
                    link = tail[row : row + 1] + tail[row + 1 : row + 2]
                    found.append(link[:, : min(bound, share - start)])
                links[mask ^ core] = found
    for half, (origins, _) in enumerate(sources_crossed(peers)(me)):
        forward_ref, backward_ref = arriving[half], arriving[2 + half]
        for index, origin in enumerate(origins):
            turn = half * (peers // 8) + index // 2
            reached = live(size_ref, 0, origin * share, share)
            backward_ref[index, 0] = live(size_ref, panel_count - 1, origin * share, share)
            masks_of = [2 * (turn + core * (peers // 4)) ^ (index % 2) for core in range(2)]
            for piece, start in enumerate(range(0, share, bound)):
                width = min(bound, share - start)
                one, two = (links[mask][piece] for mask in masks_of)
                link = jnp.where(me % 2 == 0, one, two)
                forward_ref[index, 0, :, pl.ds(start, width)] = (
                    reached[:, start : start + width] * link
                )


def part_products(ref, origins, schur_ref, products):
    side_count, share = ref.shape[2:]
    for place, origin in enumerate(origins):
        rows = pl.ds(pl.multiple_of(origin * share, share), share)
        field = ref[place].reshape(2 * side_count, share)
        terms = real_products(field, schur_ref.at[:, rows, :])
        products = terms if products is None else [a + b for a, b in zip(products, terms)]
    return products


def early_kernel(turn, sources, stage, *refs):
    products_ref = refs[-1]

    @gated(turn)
    def _():
        (mine, other), (more, _) = sources(lax.axis_index("xy"))
        if stage == 0:
            products = part_products(refs[0], mine, refs[1], None)
        else:
            products = [refs[3][part] for part in range(2)]
            products = part_products(refs[0], other, refs[2], products)
            products = part_products(refs[1], more, refs[2], products)
        for part in range(2):
            products_ref[part] = products[part]


def late_kernel(turn, sources, names, *refs):
    named = dict(zip(names, refs))
    kept_ref, message_ref = refs[-2:]

    @gated(turn)
    def _():
        origins = sources(lax.axis_index("xy"))[1][1]
        products = [named["products"][part] for part in range(2)]
        products = part_products(named["other"], origins, named["schur"], products)
        for part, value in enumerate(combined(products)):
            value = named["mask"][...] * value
            if "kept" in named:
                value = named["kept"][part] + value
            kept_ref[part] = value
            if "scale" in named:
                value = named["scale"][...] * value
            if "addend" in named:
                value = named["addend"][part] + value
            message_ref[part] = value.astype(jnp.bfloat16)


def cost_of(mine):
    _, _, side_count, share = mine.shape
    return {
        "flops": 8 * side_count * share * share * mine.shape[0],
        "moved": 4 * share * share * mine.shape[0],
    }


def first_products(turn, sources, schur, mine):
    return in_kernel(
        functools.partial(early_kernel, turn, sources, 0),
        [((2, 2 * mine.shape[2], mine.shape[3]), jnp.float32)],
        [resident(mine), resident(schur)],
        **cost_of(mine),
    )[0]


def more_products(turn, sources, pieces, schur, products):
    (_, other), (more, _) = pieces
    return in_kernel(
        functools.partial(early_kernel, turn, sources, 1),
        [(products.shape, products.dtype)],
        [resident(value) for value in (other, more, schur, products)],
        **cost_of(other),
    )[0]


def sweep_step(turn, sources, pieces, schur, products, kept, message, adds, **others):
    products = more_products(turn, sources, pieces, schur, products)
    named = {"products": products, "other": pieces[1][1], "schur": schur}
    named.update({name: value for name, value in others.items() if value is not None})
    named["kept" if adds else "old"], named["message"] = kept, message
    count = len(named)
    return in_kernel(
        functools.partial(late_kernel, turn, sources, list(named)),
        [(kept.shape, kept.dtype), (message.shape, message.dtype)],
        [resident(value) for value in named.values()],
        aliases={count - 2: 0, count - 1: 1},
        **cost_of(pieces[1][1]),
    )


def last_step(turn, sources, pieces, schur, products, mask, kepts):
    products = more_products(turn, sources, pieces, schur, products)
    operands = [products, pieces[1][1], schur, mask] + kepts
    return in_kernel(
        functools.partial(last_kernel, turn, sources),
        [
            (kepts[0].shape, kepts[0].dtype),
            ((len(kepts),) + kepts[0].shape, jnp.bfloat16),
        ],
        [resident(value) for value in operands],
        aliases={4: 0},
        **cost_of(pieces[1][1]),
    )


def last_kernel(turn, sources, products_ref, other_ref, schur_ref, mask_ref, *refs):
    kepts, kept_ref, message_ref = refs[:-2], refs[-2], refs[-1]
    for panel in range(1, len(kepts)):
        message_ref[panel] = kepts[panel][...].astype(jnp.bfloat16)

    @gated(turn)
    def _():
        origins = sources(lax.axis_index("xy"))[1][1]
        products = [products_ref[part] for part in range(2)]
        products = part_products(other_ref, origins, schur_ref, products)
        for part, value in enumerate(combined(products)):
            value = kepts[0][part] + mask_ref[...] * value
            kept_ref[part] = value
            message_ref[0, part] = value.astype(jnp.bfloat16)

    @pl.when(lax.axis_index("gz") != turn)
    def _():
        message_ref[0] = kepts[0][...].astype(jnp.bfloat16)


def pick_kernel(mine_ref, rows_ref, picked_ref):
    origins = sources_within(4 * mine_ref.shape[0])(lax.axis_index("xy"))[0][0]
    for panel, value in enumerate(picks(mine_ref, rows_ref, origins, None)):
        picked_ref[panel] = value


def picks(ref, rows_ref, origins, picked):
    _, panel_count, _, side_count, share = ref.shape
    bound = rows_ref.shape[1]
    found = []
    for panel in range(panel_count):
        total = picked[panel] if picked else jnp.zeros((2 * side_count, bound), jnp.float32)
        for place, origin in enumerate(origins):
            rows = origin * share + lax.broadcasted_iota(jnp.int32, (share, bound), 0)
            chosen = jnp.where(rows == rows_ref[pl.ds(panel, 1), :], 1.0, 0.0).astype(jnp.bfloat16)
            field = ref[place, panel].reshape(2 * side_count, share)
            total += jnp.dot(field, chosen, preferred_element_type=jnp.float32)
        found.append(total)
    return found


def inner_kernel(
    picked_ref, other_ref, more_ref, rest_ref, rows_ref, coupling_ref, inverse_ref, solved_ref, out_ref, inner_ref, sems
):
    contract = (((1,), (1,)), ((), ()))
    (_, others), (mores, rests) = sources_within(4 * other_ref.shape[0])(lax.axis_index("xy"))
    picked = [picked_ref[panel] for panel in range(picked_ref.shape[0])]
    for ref, origins in ((other_ref, others), (more_ref, mores), (rest_ref, rests)):
        picked = picks(ref, rows_ref, origins, picked)
    copies = []
    for panel, value in enumerate(picked):
        field = value.astype(jnp.bfloat16)
        lifted = combined(
            [
                lax.dot_general(
                    field, coupling_ref[panel, 0, part], contract, preferred_element_type=jnp.float32
                )
                for part in range(2)
            ]
        )
        field = jnp.concatenate(lifted).astype(jnp.bfloat16)
        back = combined(real_products(field, inverse_ref.at[panel, 0]))
        for part in range(2):
            inner_ref[panel, part] = solved_ref[panel, part] - back[part]
        copies.append(
            pltpu.make_async_copy(inner_ref.at[panel], out_ref.at[panel], sems.at[panel])
        )
        copies[-1].start()
    for copy in copies:
        copy.wait()


def on_device(
    source_inner, source_front, inner_inverse, coupling, schur_inverse, front_rows, link, front_size
):
    peers, groups = lax.axis_size("xy"), lax.axis_size("gz")
    panel_count, _, side_count, share = source_front.shape
    bound = front_rows.shape[1]
    half = peers // 4
    local = source_inner.shape[3]

    tail_rows = 2 * panel_count + 2 * -(-share // bound)
    tail_rows += -tail_rows % 16
    sent_rows = 2 * side_count * panel_count + tail_rows
    taken = [source_inner, inner_inverse, coupling, front_rows, link, source_front]
    solved, sent, _, inverse_held, coupling_held, rows_held, link_held, source_held = in_kernel(
        local_kernel,
        [
            ((panel_count, 2, side_count, local), jnp.float32),
            ((sent_rows, bound), jnp.bfloat16),
        ]
        + [(value.shape, value.dtype) for value in taken],
        [in_hbm(value) for value in taken],
        specs=[IN_HBM] * len(taken),
        scratch=[
            pltpu.VMEM((tail_rows, bound), jnp.float32),
            pltpu.SemaphoreType.DMA((len(taken) * panel_count,)),
        ],
    )
    def push(panel, shards):
        return in_kernel(
            functools.partial(push_kernel, panel, panel_count),
            [((2 * side_count, share), jnp.float32)],
            [resident(shard) for shard in shards],
            moved=2**22,
        )[0]

    shards, contrib, schurs = gathered_within(
        sent, lambda mine: push(0, [mine]), [loaded(0, schur_inverse, sent)]
    )
    (mine, other), (more, rest) = [[resident(shard) for shard in half] for half in shards]
    bases, messages = [], []
    for panel in range(panel_count):
        if panel:
            contrib, last_shards = push(panel, [mine, more, other]), [rest]
        else:
            last_shards = [more, other, rest]
        base, message = in_kernel(
            functools.partial(base_kernel, panel, panel_count),
            [((2, side_count, share), jnp.float32), ((2, side_count, share), jnp.bfloat16)],
            [front_size, resident(contrib), resident(source_held)] + last_shards,
            specs=[IN_SMEM] + [IN_VMEM] * (2 + len(last_shards)),
            moved=2**22,
        )
        bases.append(base)
        messages.append(message)

    row = ((1, share), jnp.float32)
    arriving = ((half, 1, 1, share), jnp.float32)
    scales = in_kernel(
        functools.partial(scales_kernel, panel_count, side_count),
        [row] * (3 * panel_count) + [arriving] * 4,
        [front_size, resident(link_held), mine, other, more, rest],
        specs=[IN_SMEM] + [IN_VMEM] * 5,
    )
    masks, forward_scales = scales[:panel_count], scales[panel_count : 2 * panel_count]
    backward_scales = scales[2 * panel_count : 3 * panel_count]
    arriving = scales[3 * panel_count :]

    def arrive_forward(pieces, index):
        return (arriving[index] * pieces.astype(jnp.float32)).astype(jnp.bfloat16)

    def arrive_backward(pieces, index):
        return (arriving[2 + index] * pieces.astype(jnp.float32)).astype(jnp.bfloat16)

    kept = [jnp.zeros((2, side_count, share), jnp.float32) for _ in range(panel_count)]
    within, across = sources_within(peers), sources_crossed(peers)
    order = [(turn, panel) for turn in range(groups) for panel in range(panel_count)]
    steps = [(None, 0, True)] + [step + (True,) for step in order[1:]]
    steps += [step + (False,) for step in reversed(order[:-1])]
    message = messages[0]
    for count, (turn, panel, forward) in enumerate(steps):
        if forward and panel == 0 and turn is not None:
            low, arrive = turn - 1, arrive_forward
        elif not forward and panel == panel_count - 1:
            low, arrive = turn, arrive_backward
        else:
            low = None
        sources = within if low is None else across
        if count == 1 and panel_count > 1:
            rest = [loaded(after, schur_inverse, message) for after in range(1, panel_count)]
            pieces, _, rest = gathered_within(message, lambda mine: (), rest)
            schurs += rest
            products = first_products(turn, sources, schurs[panel], pieces[0][0])
        else:
            first = functools.partial(first_products, turn, sources, schurs[panel])
            if low is not None:
                pieces, products = crossed(message, low, arrive, first)
            elif count == 0:
                beside = (bases[1:], masks, forward_scales, backward_scales, arriving)
                pieces, products, beside = gathered_within(message, first, beside)
                bases[1:], masks, forward_scales, backward_scales, arriving = beside
            else:
                pieces, products, _ = gathered_within(message, first)
        scale = addend = None
        if forward and panel < panel_count - 1:
            scale, addend = forward_scales[panel + 1], bases[panel + 1]
        elif not forward or turn == groups - 1:
            scale = backward_scales[panel]
        if count == len(steps) - 1:
            kept[0], message = last_step(turn, sources, pieces, schurs[0], products, masks[0], kept)
        else:
            kept[panel], message = sweep_step(
                turn, sources, pieces, schurs[panel], products, kept[panel], message,
                not forward or (panel == 0 and turn is not None),
                mask=masks[panel], scale=scale, addend=addend,
            )

    fronts = jnp.stack(kept)
    pick = lambda mine: in_kernel(
        pick_kernel,
        [((panel_count, 2 * side_count, bound), jnp.float32)],
        [resident(mine), resident(rows_held)],
        moved=2**22,
    )[0]
    ((_, other), (more, rest)), picked, fronts = gathered_within(message, pick, fronts)
    operands = [picked, other, more, rest, rows_held, coupling_held, inverse_held, solved]
    inner = pl.pallas_call(
        inner_kernel,
        out_shape=jax.ShapeDtypeStruct(solved.shape, jnp.float32),
        in_specs=[IN_VMEM] * len(operands),
        out_specs=IN_HBM,
        scratch_shapes=[
            pltpu.VMEM(solved.shape, jnp.float32),
            pltpu.SemaphoreType.DMA((panel_count,)),
        ],
        compiler_params=pltpu.CompilerParams(vmem_limit_bytes=16 * 2**20),
    )(*[resident(value) for value in operands])
    return inner, fronts


def solution(mesh):
    placed = (
        P("gz", None, None, "xy"),
        P("gz", None, None, "xy"),
        P("gz", "xy", None, None, None),
        P("gz", "xy", None, None, None),
        P("gz", None, None, "xy"),
        P("gz", "xy"),
        P("gz", "xy"),
        P("gz"),
    )
    return jax.shard_map(
        on_device,
        mesh=mesh,
        in_specs=placed,
        out_specs=(P("gz", None, None, "xy"), P("gz", None, None, "xy")),
        check_vma=False,
    )
```

```python
import functools

import jax
import jax.numpy as jnp
from jax import lax
from jax.experimental import pallas as pl
from jax.experimental.pallas import tpu as pltpu
from jax.sharding import PartitionSpec as P

IN_VMEM = pl.BlockSpec(memory_space=pltpu.VMEM)


IN_HBM = pl.BlockSpec(memory_space=pltpu.HBM)
IN_SMEM = pl.BlockSpec(memory_space=pltpu.SMEM)


def resident(array):
    return pltpu.with_memory_space_constraint(array, pltpu.VMEM)


def in_hbm(array):
    return pltpu.with_memory_space_constraint(array, pltpu.HBM)


def swapped(shard, mask, turn=None):
    peers, groups = lax.axis_size("xy"), lax.axis_size("gz")
    pairs = []
    for group in range(groups):
        used = mask if turn is None or (group - turn) % 2 == 0 else 1
        pairs += [(group * peers + peer, group * peers + (peer ^ used)) for peer in range(peers)]
    return lax.ppermute(shard, ("gz", "xy"), pairs)


def masks_within(peers):
    masks = [0] + list(reversed(range(2, peers, 2)))
    return masks[: peers // 4], masks[peers // 4 :]


def in_parts(one, fetched, first, beside=()):
    pieces = [(one, swapped(one, 1))]
    made = first(one)
    fetched, made, beside = lax.optimization_barrier((fetched, made, beside))
    two = jnp.stack(fetched)
    pieces.append((two, swapped(two, 1)))
    return pieces, made, beside


def gathered_within(message, turn, first, beside=()):
    one, two = [
        [swapped(message, mask, turn) if mask else message for mask in part]
        for part in masks_within(lax.axis_size("xy"))
    ]
    return in_parts(jnp.stack(one), two, first, beside)


def sources_within(peers):
    def sources(me):
        found = []
        for masks in masks_within(peers):
            mine = [me ^ mask for mask in masks]
            found.append((mine, [peer ^ 1 for peer in mine]))
        return found

    return sources


def crossed(message, low, own_scale, far_scale, first):
    peers, groups = lax.axis_size("xy"), lax.axis_size("gz")

    def across(mask):
        pairs = []
        for group in range(groups):
            for peer in range(peers):
                if group in (low, low + 1):
                    place = (2 * low + 1 - group) * peers + (peer ^ mask)
                else:
                    place = group * peers + (peer ^ 1)
                pairs.append((group * peers + peer, place))
        return lax.ppermute(message, ("gz", "xy"), pairs)

    far, near = masks_within(peers)
    own = (own_scale * across(0).astype(jnp.float32)).astype(jnp.bfloat16)
    fetched = jnp.stack([across(mask) for mask in far[1:]])
    fetched = (far_scale * fetched.astype(jnp.float32)).astype(jnp.bfloat16)
    one = jnp.concatenate([own[None], fetched])
    return in_parts(one, [swapped(own, mask) for mask in near], first)[:2]


def gated(turn):
    def wrap(body):
        if turn is None:
            body()
        else:
            pl.when(lax.axis_index("gz") == turn)(body)

    return wrap


def in_kernel(body, outs, operands, aliases=None, specs=None, scratch=(), flops=0, moved=0):
    return pl.pallas_call(
        body,
        out_shape=tuple(pltpu.VMEM(shape, dtype) for shape, dtype in outs),
        in_specs=specs or [IN_VMEM] * len(operands),
        out_specs=(IN_VMEM,) * len(outs),
        scratch_shapes=scratch,
        input_output_aliases=aliases or {},
        compiler_params=pltpu.CompilerParams(vmem_limit_bytes=16 * 2**20),
        cost_estimate=pl.CostEstimate(flops=flops, bytes_accessed=moved, transcendentals=0),
    )(*operands)


def real_products(field, matrix):
    return [
        jnp.dot(field, matrix[part], preferred_element_type=jnp.float32) for part in range(2)
    ]


def combined(products):
    first, second = products
    count = first.shape[0] // 2
    return first[:count] - second[count:], second[:count] + first[count:]


def panel_copies(panel, schur_ref, out_ref, sems):
    chunks = sems.shape[0] // 2
    rows = schur_ref.shape[2] // chunks
    copies = []
    for part in range(2):
        for chunk in range(chunks):
            span = pl.ds(chunk * rows, rows)
            copies.append(
                pltpu.make_async_copy(
                    schur_ref.at[panel, part, span, :],
                    out_ref.at[part, span, :],
                    sems.at[part * chunks + chunk],
                )
            )
    for copy in copies:
        copy.start()
    return copies


def load_kernel(schur_ref, after_ref, out_ref, sems):
    del after_ref
    for copy in panel_copies(0, schur_ref, out_ref, sems):
        copy.wait()


def loaded(schur, after):
    return in_kernel(
        load_kernel,
        [(schur.shape[1:], schur.dtype)],
        [in_hbm(schur), after],
        specs=[IN_HBM, pl.BlockSpec(memory_space=pl.ANY)],
        scratch=[pltpu.SemaphoreType.DMA((8,))],
        moved=schur.dtype.itemsize * schur[0].size,
    )[0]


def local_kernel(*refs):
    operands, size_in, (solved_ref, sent_ref), held = refs[:6], refs[6], refs[7:9], refs[9:15]
    rows_out, (far_first, far_last), (sizes, tail_ref, sems) = refs[15:-5], refs[-5:-3], refs[-3:]
    source_ref, inverse_ref, coupling_ref, rows_ref, link_ref, _ = held
    panel_count, _, side_count, _ = source_ref.shape
    bound, share = sent_ref.shape[1], link_ref.shape[1]
    copies = []
    for index, (operand, place) in enumerate(zip(operands, held)):
        for panel in range(panel_count):
            copies.append(
                pltpu.make_async_copy(
                    operand.at[panel], place.at[panel], sems.at[index * panel_count + panel]
                )
            )
    by_operand = [copies[i * panel_count : (i + 1) * panel_count] for i in range(len(operands))]
    size_copy = pltpu.make_async_copy(size_in, sizes, sems.at[len(copies)])
    size_copy.start()
    for panel in range(panel_count):
        for index in range(3):
            by_operand[index][panel].start()
    for group in by_operand[3:]:
        for copy in group:
            copy.start()
    for panel in range(panel_count):
        by_operand[0][panel].wait()
        by_operand[1][panel].wait()
        field = source_ref[panel].astype(jnp.bfloat16).reshape(2 * side_count, -1)
        solved = combined(real_products(field, inverse_ref.at[panel, 0]))
        for part in range(2):
            solved_ref[panel, part] = solved[part]
        field = jnp.concatenate(solved).astype(jnp.bfloat16)
        by_operand[2][panel].wait()
        pushed = combined(real_products(field, coupling_ref.at[panel, 0]))
        for part in range(2):
            start = (2 * panel + part) * side_count
            sent_ref[pl.ds(start, side_count), :] = pushed[part].astype(jnp.bfloat16)
    for group in by_operand[3:]:
        for copy in group:
            copy.wait()
    tail_ref[...] = jnp.zeros(tail_ref.shape, jnp.float32)
    for panel in range(panel_count):
        rows = rows_ref[pl.ds(panel, 1), :]
        tail_ref[pl.ds(panel, 1), :] = (rows >> 8).astype(jnp.float32)
        tail_ref[pl.ds(panel_count + panel, 1), :] = (rows & 255).astype(jnp.float32)
    row = 2 * panel_count
    for start in range(0, share, bound):
        width = min(bound, share - start)
        link = link_ref[pl.ds(0, 1), pl.ds(start, width)]
        high = link.astype(jnp.bfloat16).astype(jnp.float32)
        tail_ref[pl.ds(row, 1), pl.ds(0, width)] = high
        tail_ref[pl.ds(row + 1, 1), pl.ds(0, width)] = link - high
        row += 2
    first = 2 * side_count * panel_count
    sent_ref[pl.ds(first, tail_ref.shape[0]), :] = tail_ref[...].astype(jnp.bfloat16)
    size_copy.wait()
    me = lax.axis_index("xy")
    masks = [live(sizes, panel, me * share, share) for panel in range(panel_count)]
    for panel in range(panel_count):
        link = link_ref[pl.ds(panel, 1), :]
        rows_out[panel][...] = masks[panel]
        rows_out[panel_count + panel][...] = masks[panel] * link
        rows_out[2 * panel_count + panel][...] = link * masks[panel - 1] if panel else link
    for index, mask in enumerate(masks_within(4 * (1 + far_first.shape[0]))[0][1:]):
        start = (me ^ mask) * share
        far_first[index, 0] = live(sizes, 0, start, share)
        far_last[index, 0] = live(sizes, panel_count - 1, start, share)


def tail_of(ref, place, first):
    return ref[place, pl.ds(first, ref.shape[1] - first), :].astype(jnp.float32)


def live(size_ref, panel, start, share):
    rows = start + lax.broadcasted_iota(jnp.int32, (1, share), 1)
    return jnp.where(rows < size_ref[panel], 1.0, 0.0)


def pushed_up(panel, panel_count, count, share, refs, contrib):
    bound = refs[0].shape[2]
    own_rows = lax.axis_index("xy") * share + lax.broadcasted_iota(jnp.int32, (share, bound), 0)
    contract = (((1,), (1,)), ((), ()))
    for ref in refs:
        for place in range(ref.shape[0]):
            values = ref[place, pl.ds(count * panel, count), :]
            tail = tail_of(ref, place, count * panel_count)
            high = tail[panel : panel + 1]
            low = tail[panel_count + panel : panel_count + panel + 1]
            places = (256.0 * high + low).astype(jnp.int32)
            hits = jnp.where(own_rows == places, 1.0, 0.0).astype(jnp.bfloat16)
            contrib += lax.dot_general(values, hits, contract, preferred_element_type=jnp.float32)
    return contrib


def push_kernel(panel, panel_count, parts, *refs):
    contrib_ref = refs[-1]
    count, share = contrib_ref.shape
    contrib = refs[parts][...] if len(refs) > parts + 1 else jnp.zeros((count, share), jnp.float32)
    contrib_ref[...] = pushed_up(panel, panel_count, count, share, refs[:parts], contrib)


def base_kernel(panel, panel_count, mask_ref, contrib_ref, source_ref, *refs):
    refs, base_ref, message_ref = refs[:-2], refs[-2], refs[-1]
    _, side_count, share = base_ref.shape
    count = 2 * side_count
    contrib = pushed_up(panel, panel_count, count, share, refs, contrib_ref[...])
    for part in range(2):
        rows = slice(part * side_count, (part + 1) * side_count)
        base = mask_ref[...] * (source_ref[panel, part] - contrib[rows])
        base_ref[part] = base
        message_ref[part] = base.astype(jnp.bfloat16)


def later_kernel(panel, panel_count, mask_ref, source_ref, *refs):
    shards, schur_ref, base_ref, out_ref, sems = refs[:4], refs[4], refs[6], refs[7], refs[8]
    copies = panel_copies(panel, schur_ref, out_ref, sems)
    _, side_count, share = base_ref.shape
    count = 2 * side_count
    zeros = jnp.zeros((count, share), jnp.float32)
    contrib = pushed_up(panel, panel_count, count, share, shards, zeros)
    for part in range(2):
        rows = slice(part * side_count, (part + 1) * side_count)
        base_ref[part] = mask_ref[...] * (source_ref[panel, part] - contrib[rows])
    for copy in copies:
        copy.wait()


def far_kernel(panel_count, side_count, mask_ref, far_ref, scale_ref):
    share, bound = scale_ref.shape[3], far_ref.shape[2]
    for index in range(scale_ref.shape[0]):
        tail = tail_of(far_ref, 1 + index, 2 * side_count * panel_count)
        for piece, place in enumerate(range(0, share, bound)):
            columns = pl.ds(place, min(bound, share - place))
            row = 2 * (panel_count + piece)
            link = (tail[row : row + 1] + tail[row + 1 : row + 2])[:, : columns.size]
            scale_ref[index, 0, :, columns] = mask_ref[index, 0, :, columns] * link


def part_products(ref, origins, schur_ref, products):
    side_count, share = ref.shape[2:]
    for place, origin in enumerate(origins):
        rows = pl.ds(pl.multiple_of(origin * share, share), share)
        field = ref[place].reshape(2 * side_count, share)
        terms = real_products(field, schur_ref.at[:, rows, :])
        products = terms if products is None else [a + b for a, b in zip(products, terms)]
    return products


def products_kernel(turn, sources, which, *refs):
    schur_ref, products_ref = refs[len(which)], refs[-1]

    @gated(turn)
    def _():
        origins = sources(lax.axis_index("xy"))
        products = None
        if len(refs) > len(which) + 2:
            products = [refs[len(which) + 1][part] for part in range(2)]
        for ref, (part, core) in zip(refs, which):
            products = part_products(ref, origins[part][core], schur_ref, products)
        for part in range(2):
            products_ref[part] = products[part]


def late_kernel(turn, sources, names, *refs):
    named = dict(zip(names, refs))
    kept_ref, message_ref = refs[-2:]

    @gated(turn)
    def _():
        origins = sources(lax.axis_index("xy"))[-1][1]
        products = [named["products"][part] for part in range(2)]
        products = part_products(named["other"], origins, named["schur"], products)
        for part, value in enumerate(combined(products)):
            value = named["mask"][...] * value
            if "kept" in named:
                value = named["kept"][part] + value
            kept_ref[part] = value
            if "scale" in named:
                value = named["scale"][...] * value
            if "addend" in named:
                value = named["addend"][part] + value
            message_ref[part] = value.astype(jnp.bfloat16)


def cost_of(mine):
    _, _, side_count, share = mine.shape
    return {
        "flops": 8 * side_count * share * share * mine.shape[0],
        "moved": 4 * share * share * mine.shape[0],
    }


def products_of(turn, sources, which, parts, schur, products=None):
    side_count, share = parts[0].shape[2:]
    operands = [*parts, schur] + ([] if products is None else [products])
    return in_kernel(
        functools.partial(products_kernel, turn, sources, which),
        [((2, 2 * side_count, share), jnp.float32)],
        [resident(value) for value in operands],
        **cost_of(parts[0]),
    )[0]


def first_products(turn, sources, schur, mine):
    return products_of(turn, sources, [(0, 0)], [mine], schur)


def more_products(turn, sources, pieces, schur, products):
    (_, other), (more, _) = pieces
    return products_of(turn, sources, [(0, 1), (1, 0)], [other, more], schur, products)


def sweep_step(turn, sources, pieces, schur, products, kept, message, adds, **others):
    products = more_products(turn, sources, pieces, schur, products)
    named = {"products": products, "other": pieces[-1][1], "schur": schur}
    named.update({name: value for name, value in others.items() if value is not None})
    named["kept" if adds else "old"], named["message"] = kept, message
    count = len(named)
    return in_kernel(
        functools.partial(late_kernel, turn, sources, list(named)),
        [(kept.shape, kept.dtype), (message.shape, message.dtype)],
        [resident(value) for value in named.values()],
        aliases={count - 2: 0, count - 1: 1},
        **cost_of(pieces[-1][1]),
    )


def last_step(turn, sources, pieces, schur, products, mask, kepts):
    products = more_products(turn, sources, pieces, schur, products)
    operands = [products, pieces[-1][1], schur, mask] + kepts
    return in_kernel(
        functools.partial(last_kernel, turn, sources),
        [
            (kepts[0].shape, kepts[0].dtype),
            ((len(kepts),) + kepts[0].shape, jnp.bfloat16),
        ],
        [resident(value) for value in operands],
        aliases={4: 0},
        **cost_of(pieces[-1][1]),
    )


def last_kernel(turn, sources, products_ref, other_ref, schur_ref, mask_ref, *refs):
    kepts, kept_ref, message_ref = refs[:-2], refs[-2], refs[-1]
    for panel in range(1, len(kepts)):
        message_ref[panel] = kepts[panel][...].astype(jnp.bfloat16)

    @gated(turn)
    def _():
        origins = sources(lax.axis_index("xy"))[-1][1]
        products = [products_ref[part] for part in range(2)]
        products = part_products(other_ref, origins, schur_ref, products)
        for part, value in enumerate(combined(products)):
            value = kepts[0][part] + mask_ref[...] * value
            kept_ref[part] = value
            message_ref[0, part] = value.astype(jnp.bfloat16)

    @pl.when(lax.axis_index("gz") != turn)
    def _():
        message_ref[0] = kepts[0][...].astype(jnp.bfloat16)


def pick_kernel(sources, which, *refs):
    rows_ref, picked_ref = refs[len(which)], refs[-1]
    origins = sources(lax.axis_index("xy"))
    picked = None
    if len(refs) > len(which) + 2:
        picked = [refs[len(which) + 1][panel] for panel in range(picked_ref.shape[0])]
    for ref, (part, core) in zip(refs, which):
        picked = picks(ref, rows_ref, origins[part][core], picked)
    for panel, value in enumerate(picked):
        picked_ref[panel] = value


def picks(ref, rows_ref, origins, picked):
    _, panel_count, _, side_count, share = ref.shape
    bound = rows_ref.shape[1]
    found = []
    for panel in range(panel_count):
        total = picked[panel] if picked else jnp.zeros((2 * side_count, bound), jnp.float32)
        for place, origin in enumerate(origins):
            rows = origin * share + lax.broadcasted_iota(jnp.int32, (share, bound), 0)
            chosen = jnp.where(rows == rows_ref[pl.ds(panel, 1), :], 1.0, 0.0).astype(jnp.bfloat16)
            field = ref[place, panel].reshape(2 * side_count, share)
            total += jnp.dot(field, chosen, preferred_element_type=jnp.float32)
        found.append(total)
    return found


def inner_kernel(
    sources, picked_ref, last_ref, rows_ref, coupling_ref, inverse_ref, solved_ref, out_ref, inner_ref, sems
):
    contract = (((1,), (1,)), ((), ()))
    origins = sources(lax.axis_index("xy"))[-1][1]
    picked = picks(last_ref, rows_ref, origins, [picked_ref[p] for p in range(picked_ref.shape[0])])
    lifted = [
        combined(
            [
                lax.dot_general(
                    value.astype(jnp.bfloat16),
                    coupling_ref[panel, 0, part],
                    contract,
                    preferred_element_type=jnp.float32,
                )
                for part in range(2)
            ]
        )
        for panel, value in enumerate(picked)
    ]
    copies = []
    for panel, value in enumerate(lifted):
        field = jnp.concatenate(value).astype(jnp.bfloat16)
        back = combined(real_products(field, inverse_ref.at[panel, 0]))
        for part in range(2):
            inner_ref[panel, part] = solved_ref[panel, part] - back[part]
        copies.append(
            pltpu.make_async_copy(inner_ref.at[panel], out_ref.at[panel], sems.at[panel])
        )
        copies[-1].start()
    for copy in copies:
        copy.wait()


def on_device(
    source_inner, source_front, inner_inverse, coupling, schur_inverse, front_rows, link, front_size
):
    peers, groups = lax.axis_size("xy"), lax.axis_size("gz")
    panel_count, _, side_count, share = source_front.shape
    bound = front_rows.shape[1]
    local = source_inner.shape[3]

    tail_rows = 2 * panel_count + 2 * -(-share // bound)
    tail_rows += -tail_rows % 16
    sent_rows = 2 * side_count * panel_count + tail_rows
    taken = [source_inner, inner_inverse, coupling, front_rows, link, source_front]
    row = ((1, share), jnp.float32)
    arriving = ((peers // 4 - 1, 1, 1, share), jnp.float32)
    solved, sent, _, inverse_held, coupling_held, rows_held, _, source_held, *scales = in_kernel(
        local_kernel,
        [
            ((panel_count, 2, side_count, local), jnp.float32),
            ((sent_rows, bound), jnp.bfloat16),
        ]
        + [(value.shape, value.dtype) for value in taken]
        + [row] * (3 * panel_count)
        + [arriving] * 2,
        [in_hbm(value) for value in taken + [front_size]],
        specs=[IN_HBM] * (len(taken) + 1),
        scratch=[
            pltpu.SMEM(front_size.shape, jnp.int32),
            pltpu.VMEM((tail_rows, bound), jnp.float32),
            pltpu.SemaphoreType.DMA((len(taken) * panel_count + 1,)),
        ],
    )
    masks, forward_scales = scales[:panel_count], scales[panel_count : 2 * panel_count]
    backward_scales, far_scales = scales[2 * panel_count : 3 * panel_count], scales[3 * panel_count :]

    def push(panel, shards, contrib=None):
        operands = shards + ([] if contrib is None else [contrib])
        return in_kernel(
            functools.partial(push_kernel, panel, panel_count, len(shards)),
            [((2 * side_count, share), jnp.float32)],
            [resident(value) for value in operands],
            moved=2**22,
        )[0]

    shards, contrib, schurs = gathered_within(
        sent, None, lambda mine: push(0, [mine]), [loaded(schur_inverse, sent)]
    )
    shards = [shard for part in shards for shard in part]
    contrib = push(0, shards[1:3], contrib)
    operands = [masks[0], contrib, source_held, shards[3]]
    base, message = in_kernel(
        functools.partial(base_kernel, 0, panel_count),
        [((2, side_count, share), jnp.float32), ((2, side_count, share), jnp.bfloat16)],
        [resident(value) for value in operands],
        moved=2**22,
    )
    bases = [base]
    for panel in range(1, panel_count):
        operands = [resident(value) for value in (masks[panel], source_held, *shards)]
        base, schur = in_kernel(
            functools.partial(later_kernel, panel, panel_count),
            [((2, side_count, share), jnp.float32), (schur_inverse.shape[1:], schur_inverse.dtype)],
            operands + [in_hbm(schur_inverse), message],
            specs=[IN_VMEM] * len(operands) + [IN_HBM, pl.BlockSpec(memory_space=pl.ANY)],
            scratch=[pltpu.SemaphoreType.DMA((8,))],
            moved=2**23,
        )
        bases.append(base)
        schurs.append(schur)
    far_scales[0] = in_kernel(
        functools.partial(far_kernel, panel_count, side_count),
        [arriving],
        [resident(far_scales[0]), resident(shards[0])],
    )[0]

    kept = [jnp.zeros((2, side_count, share), jnp.float32) for _ in range(panel_count)]
    sources = sources_within(peers)
    order = [(turn, panel) for turn in range(groups) for panel in range(panel_count)]
    steps = [(None, 0, True)] + [step + (True,) for step in order[1:]]
    steps += [step + (False,) for step in reversed(order[:-1])]
    for count, (turn, panel, forward) in enumerate(steps):
        if forward and panel == 0 and turn is not None:
            low, own_scale, far_scale = turn - 1, forward_scales[0], far_scales[0]
        elif not forward and panel == panel_count - 1:
            low, own_scale, far_scale = turn, masks[panel], far_scales[1]
        else:
            low = None
        first = functools.partial(first_products, turn, sources, schurs[panel])
        if low is not None:
            pieces, products = crossed(message, low, own_scale, far_scale, first)
        elif count == 0:
            beside = (bases[1:], schurs[1:], far_scales)
            pieces, products, beside = gathered_within(message, None, first, beside)
            bases[1:], schurs[1:], far_scales = beside
        else:
            pieces, products, _ = gathered_within(message, turn, first)
        scale = addend = None
        if forward and panel < panel_count - 1:
            scale, addend = forward_scales[panel + 1], bases[panel + 1]
        elif not forward or turn == groups - 1:
            scale = backward_scales[panel]
        if count == len(steps) - 1:
            kept[0], message = last_step(turn, sources, pieces, schurs[0], products, masks[0], kept)
        else:
            kept[panel], message = sweep_step(
                turn, sources, pieces, schurs[panel], products, kept[panel], message,
                not forward or (panel == 0 and turn is not None),
                mask=masks[panel], scale=scale, addend=addend,
            )

    fronts = jnp.stack(kept)

    def pick(which, parts, *picked):
        return in_kernel(
            functools.partial(pick_kernel, sources, which),
            [((panel_count, 2 * side_count, bound), jnp.float32)],
            [resident(value) for value in (*parts, rows_held, *picked)],
            moved=2**22,
        )[0]

    pieces, picked, _ = gathered_within(message, None, lambda mine: pick([(0, 0)], [mine]))
    (_, other), (more, last) = pieces
    picked = pick([(0, 1), (1, 0)], [other, more], picked)
    operands = [picked, last, rows_held, coupling_held, inverse_held, solved]
    inner = pl.pallas_call(
        functools.partial(inner_kernel, sources),
        out_shape=jax.ShapeDtypeStruct(solved.shape, jnp.float32),
        in_specs=[IN_VMEM] * len(operands),
        out_specs=IN_HBM,
        scratch_shapes=[
            pltpu.VMEM(solved.shape, jnp.float32),
            pltpu.SemaphoreType.DMA((panel_count,)),
        ],
        compiler_params=pltpu.CompilerParams(vmem_limit_bytes=16 * 2**20),
    )(*[resident(value) for value in operands])
    return inner, fronts


def solution(mesh):
    placed = (
        P("gz", None, None, "xy"),
        P("gz", None, None, "xy"),
        P("gz", "xy", None, None, None),
        P("gz", "xy", None, None, None),
        P("gz", None, None, "xy"),
        P("gz", "xy"),
        P("gz", "xy"),
        P("gz"),
    )
    return jax.shard_map(
        on_device,
        mesh=mesh,
        in_specs=placed,
        out_specs=(P("gz", None, None, "xy"), P("gz", None, None, "xy")),
        check_vma=False,
    )
```

```python
import functools

import jax
import jax.numpy as jnp
from jax import lax
from jax.experimental import pallas as pl
from jax.experimental.pallas import tpu as pltpu
from jax.sharding import PartitionSpec as P

IN_VMEM = pl.BlockSpec(memory_space=pltpu.VMEM)


IN_HBM = pl.BlockSpec(memory_space=pltpu.HBM)
IN_SMEM = pl.BlockSpec(memory_space=pltpu.SMEM)


def resident(array):
    return pltpu.with_memory_space_constraint(array, pltpu.VMEM)


def in_hbm(array):
    return pltpu.with_memory_space_constraint(array, pltpu.HBM)


def swapped(shard, mask, turn=None):
    peers, groups = lax.axis_size("xy"), lax.axis_size("gz")
    pairs = []
    for group in range(groups):
        used = mask if turn is None or (group - turn) % 2 == 0 else 1
        pairs += [(group * peers + peer, group * peers + (peer ^ used)) for peer in range(peers)]
    return lax.ppermute(shard, ("gz", "xy"), pairs)


def masks_within(peers):
    masks = [0] + list(reversed(range(2, peers, 2)))
    return masks[: peers // 4], masks[peers // 4 :]


def in_parts(one, fetched, first, beside=(), join=jnp.stack):
    pieces = [(one, swapped(one, 1))]
    made = first(one)
    fetched, made, beside = lax.optimization_barrier((fetched, made, beside))
    two = join(fetched)
    pieces.append((two, swapped(two, 1)))
    return pieces, made, beside


def gathered_within(message, turn, first, beside=()):
    one, two = [
        [swapped(message, mask, turn) if mask else message for mask in part]
        for part in masks_within(lax.axis_size("xy"))
    ]
    return in_parts(jnp.stack(one), two, first, beside)


def sources_by(parts):
    def sources(me):
        found = []
        for masks in parts:
            mine = [me ^ mask for mask in masks]
            found.append((mine, [peer ^ 1 for peer in mine]))
        return found

    return sources


def masks_across(peers):
    masks = list(reversed(range(0, peers, 2)))
    return masks[: peers // 4], masks[peers // 4 :]


def crossed(message, low, by, scales, first):
    peers, groups = lax.axis_size("xy"), lax.axis_size("gz")

    def across(mask):
        pairs = []
        for group in range(groups):
            lower = group if (group - low) % 2 == 0 else group - 1
            joined = 0 <= lower and lower + 1 < groups
            for peer in range(peers):
                if mask == 0:
                    place = (2 * lower + 1 - group) * peers + peer if joined else group * peers + (peer ^ 1)
                elif joined and group == (lower if by > 0 else lower + 1):
                    place = (group + by) * peers + (peer ^ mask)
                else:
                    continue
                pairs.append((group * peers + peer, place))
        return lax.ppermute(message, ("gz", "xy"), pairs)

    def scaled(part, scale):
        return (scale * jnp.stack(part).astype(jnp.float32)).astype(jnp.bfloat16)

    one, two = [[across(mask) for mask in part] for part in masks_across(peers)]
    join = functools.partial(scaled, scale=scales[1])
    return in_parts(scaled(one, scales[0]), two, first, join=join)[:2]


def gated(turn):
    def wrap(body):
        if turn is None:
            body()
        else:
            pl.when(lax.axis_index("gz") == turn)(body)

    return wrap


def in_kernel(body, outs, operands, aliases=None, specs=None, scratch=(), flops=0, moved=0):
    return pl.pallas_call(
        body,
        out_shape=tuple(pltpu.VMEM(shape, dtype) for shape, dtype in outs),
        in_specs=specs or [IN_VMEM] * len(operands),
        out_specs=(IN_VMEM,) * len(outs),
        scratch_shapes=scratch,
        input_output_aliases=aliases or {},
        compiler_params=pltpu.CompilerParams(vmem_limit_bytes=16 * 2**20),
        cost_estimate=pl.CostEstimate(flops=flops, bytes_accessed=moved, transcendentals=0),
    )(*operands)


def real_products(field, matrix):
    return [
        jnp.dot(field, matrix[part], preferred_element_type=jnp.float32) for part in range(2)
    ]


def combined(products):
    first, second = products
    count = first.shape[0] // 2
    return first[:count] - second[count:], second[:count] + first[count:]


def panel_copies(panel, schur_ref, out_ref, sems):
    chunks = sems.shape[0] // 2
    rows = schur_ref.shape[2] // chunks
    copies = []
    for part in range(2):
        for chunk in range(chunks):
            span = pl.ds(chunk * rows, rows)
            copies.append(
                pltpu.make_async_copy(
                    schur_ref.at[panel, part, span, :],
                    out_ref.at[part, span, :],
                    sems.at[part * chunks + chunk],
                )
            )
    for copy in copies:
        copy.start()
    return copies


def load_kernel(schur_ref, after_ref, out_ref, sems):
    del after_ref
    for copy in panel_copies(0, schur_ref, out_ref, sems):
        copy.wait()


def loaded(schur, after):
    return in_kernel(
        load_kernel,
        [(schur.shape[1:], schur.dtype)],
        [in_hbm(schur), after],
        specs=[IN_HBM, pl.BlockSpec(memory_space=pl.ANY)],
        scratch=[pltpu.SemaphoreType.DMA((8,))],
        moved=schur.dtype.itemsize * schur[0].size,
    )[0]


def local_kernel(*refs):
    operands, size_in, (solved_ref, sent_ref), held = refs[:6], refs[6], refs[7:9], refs[9:15]
    rows_out, met, (sizes, tail_ref, sems) = refs[15:-7], refs[-7:-3], refs[-3:]
    source_ref, inverse_ref, coupling_ref, rows_ref, link_ref, _ = held
    panel_count, _, side_count, _ = source_ref.shape
    bound, share = sent_ref.shape[1], link_ref.shape[1]
    copies = []
    for index, (operand, place) in enumerate(zip(operands, held)):
        for panel in range(panel_count):
            copies.append(
                pltpu.make_async_copy(
                    operand.at[panel], place.at[panel], sems.at[index * panel_count + panel]
                )
            )
    by_operand = [copies[i * panel_count : (i + 1) * panel_count] for i in range(len(operands))]
    size_copy = pltpu.make_async_copy(size_in, sizes, sems.at[len(copies)])
    size_copy.start()
    for panel in range(panel_count):
        for index in range(3):
            by_operand[index][panel].start()
    for group in by_operand[3:]:
        for copy in group:
            copy.start()
    for panel in range(panel_count):
        by_operand[0][panel].wait()
        by_operand[1][panel].wait()
        field = source_ref[panel].astype(jnp.bfloat16).reshape(2 * side_count, -1)
        solved = combined(real_products(field, inverse_ref.at[panel, 0]))
        for part in range(2):
            solved_ref[panel, part] = solved[part]
        field = jnp.concatenate(solved).astype(jnp.bfloat16)
        by_operand[2][panel].wait()
        pushed = combined(real_products(field, coupling_ref.at[panel, 0]))
        for part in range(2):
            start = (2 * panel + part) * side_count
            sent_ref[pl.ds(start, side_count), :] = pushed[part].astype(jnp.bfloat16)
    for group in by_operand[3:]:
        for copy in group:
            copy.wait()
    tail_ref[...] = jnp.zeros(tail_ref.shape, jnp.float32)
    for panel in range(panel_count):
        rows = rows_ref[pl.ds(panel, 1), :]
        tail_ref[pl.ds(panel, 1), :] = (rows >> 8).astype(jnp.float32)
        tail_ref[pl.ds(panel_count + panel, 1), :] = (rows & 255).astype(jnp.float32)
    row = 2 * panel_count
    for start in range(0, share, bound):
        width = min(bound, share - start)
        link = link_ref[pl.ds(0, 1), pl.ds(start, width)]
        high = link.astype(jnp.bfloat16).astype(jnp.float32)
        tail_ref[pl.ds(row, 1), pl.ds(0, width)] = high
        tail_ref[pl.ds(row + 1, 1), pl.ds(0, width)] = link - high
        row += 2
    first = 2 * side_count * panel_count
    sent_ref[pl.ds(first, tail_ref.shape[0]), :] = tail_ref[...].astype(jnp.bfloat16)
    size_copy.wait()
    me = lax.axis_index("xy")
    masks = [live(sizes, panel, me * share, share) for panel in range(panel_count)]
    for panel in range(panel_count):
        link = link_ref[pl.ds(panel, 1), :]
        rows_out[panel][...] = masks[panel]
        rows_out[panel_count + panel][...] = masks[panel] * link
        rows_out[2 * panel_count + panel][...] = link * masks[panel - 1] if panel else link
    for half, part in enumerate(masks_across(4 * met[0].shape[0])):
        for index, mask in enumerate(part):
            start = (me ^ mask) * share
            met[half][index, 0] = live(sizes, 0, start, share)
            met[2 + half][index, 0] = live(sizes, panel_count - 1, start, share)


def tail_of(ref, place, first):
    return ref[place, pl.ds(first, ref.shape[1] - first), :].astype(jnp.float32)


def live(size_ref, panel, start, share):
    rows = start + lax.broadcasted_iota(jnp.int32, (1, share), 1)
    return jnp.where(rows < size_ref[panel], 1.0, 0.0)


def pushed_up(panel, panel_count, count, share, refs, contrib):
    bound = refs[0].shape[2]
    own_rows = lax.axis_index("xy") * share + lax.broadcasted_iota(jnp.int32, (share, bound), 0)
    contract = (((1,), (1,)), ((), ()))
    for ref in refs:
        for place in range(ref.shape[0]):
            values = ref[place, pl.ds(count * panel, count), :]
            tail = tail_of(ref, place, count * panel_count)
            high = tail[panel : panel + 1]
            low = tail[panel_count + panel : panel_count + panel + 1]
            places = (256.0 * high + low).astype(jnp.int32)
            hits = jnp.where(own_rows == places, 1.0, 0.0).astype(jnp.bfloat16)
            contrib += lax.dot_general(values, hits, contract, preferred_element_type=jnp.float32)
    return contrib


def push_kernel(panel, panel_count, parts, *refs):
    contrib_ref = refs[-1]
    count, share = contrib_ref.shape
    contrib = refs[parts][...] if len(refs) > parts + 1 else jnp.zeros((count, share), jnp.float32)
    contrib_ref[...] = pushed_up(panel, panel_count, count, share, refs[:parts], contrib)


def base_kernel(panel, panel_count, mask_ref, contrib_ref, source_ref, *refs):
    refs, base_ref, message_ref = refs[:-2], refs[-2], refs[-1]
    _, side_count, share = base_ref.shape
    count = 2 * side_count
    contrib = pushed_up(panel, panel_count, count, share, refs, contrib_ref[...])
    for part in range(2):
        rows = slice(part * side_count, (part + 1) * side_count)
        base = mask_ref[...] * (source_ref[panel, part] - contrib[rows])
        base_ref[part] = base
        message_ref[part] = base.astype(jnp.bfloat16)


def later_kernel(panel, panel_count, mask_ref, source_ref, *refs):
    shards, schur_ref, base_ref, out_ref, sems = refs[:4], refs[4], refs[6], refs[7], refs[8]
    copies = panel_copies(panel, schur_ref, out_ref, sems)
    _, side_count, share = base_ref.shape
    count = 2 * side_count
    zeros = jnp.zeros((count, share), jnp.float32)
    contrib = pushed_up(panel, panel_count, count, share, shards, zeros)
    for part in range(2):
        rows = slice(part * side_count, (part + 1) * side_count)
        base_ref[part] = mask_ref[...] * (source_ref[panel, part] - contrib[rows])
    for copy in copies:
        copy.wait()


def link_kernel(panel_count, side_count, one_mask, two_mask, one_ref, two_ref, one_out, two_out):
    share, bound = one_out.shape[3], one_ref.shape[2]
    peers = 4 * one_out.shape[0]
    tails = {}
    for ref, part in zip((one_ref, two_ref), masks_within(peers)):
        for index, mask in enumerate(part):
            tails[mask] = tail_of(ref, index, 2 * side_count * panel_count)
    for mask_ref, out, part in zip((one_mask, two_mask), (one_out, two_out), masks_across(peers)):
        for index, mask in enumerate(part):
            for piece, place in enumerate(range(0, share, bound)):
                columns = pl.ds(place, min(bound, share - place))
                row = 2 * (panel_count + piece)
                link = tails[mask][row : row + 1] + tails[mask][row + 1 : row + 2]
                out[index, 0, :, columns] = mask_ref[index, 0, :, columns] * link[:, : columns.size]


def part_products(ref, origins, schur_ref, products):
    side_count, share = ref.shape[2:]
    for place, origin in enumerate(origins):
        rows = pl.ds(pl.multiple_of(origin * share, share), share)
        field = ref[place].reshape(2 * side_count, share)
        terms = real_products(field, schur_ref.at[:, rows, :])
        products = terms if products is None else [a + b for a, b in zip(products, terms)]
    return products


def products_kernel(turn, sources, which, *refs):
    schur_ref, products_ref = refs[len(which)], refs[-1]

    @gated(turn)
    def _():
        origins = sources(lax.axis_index("xy"))
        products = None
        if len(refs) > len(which) + 2:
            products = [refs[len(which) + 1][part] for part in range(2)]
        for ref, (part, core) in zip(refs, which):
            products = part_products(ref, origins[part][core], schur_ref, products)
        for part in range(2):
            products_ref[part] = products[part]


def late_kernel(turn, sources, names, *refs):
    named = dict(zip(names, refs))
    kept_ref, message_ref = refs[-2:]

    @gated(turn)
    def _():
        origins = sources(lax.axis_index("xy"))[-1][1]
        products = [named["products"][part] for part in range(2)]
        products = part_products(named["other"], origins, named["schur"], products)
        for part, value in enumerate(combined(products)):
            value = named["mask"][...] * value
            if "kept" in named:
                value = named["kept"][part] + value
            kept_ref[part] = value
            if "scale" in named:
                value = named["scale"][...] * value
            if "addend" in named:
                value = named["addend"][part] + value
            message_ref[part] = value.astype(jnp.bfloat16)


def cost_of(mine):
    _, _, side_count, share = mine.shape
    return {
        "flops": 8 * side_count * share * share * mine.shape[0],
        "moved": 4 * share * share * mine.shape[0],
    }


def products_of(turn, sources, which, parts, schur, products=None):
    side_count, share = parts[0].shape[2:]
    operands = [*parts, schur] + ([] if products is None else [products])
    return in_kernel(
        functools.partial(products_kernel, turn, sources, which),
        [((2, 2 * side_count, share), jnp.float32)],
        [resident(value) for value in operands],
        **cost_of(parts[0]),
    )[0]


def first_products(turn, sources, schur, mine):
    return products_of(turn, sources, [(0, 0)], [mine], schur)


def more_products(turn, sources, pieces, schur, products):
    (_, other), (more, _) = pieces
    return products_of(turn, sources, [(0, 1), (1, 0)], [other, more], schur, products)


def sweep_step(turn, sources, pieces, schur, products, kept, message, adds, **others):
    products = more_products(turn, sources, pieces, schur, products)
    named = {"products": products, "other": pieces[-1][1], "schur": schur}
    named.update({name: value for name, value in others.items() if value is not None})
    named["kept" if adds else "old"], named["message"] = kept, message
    count = len(named)
    return in_kernel(
        functools.partial(late_kernel, turn, sources, list(named)),
        [(kept.shape, kept.dtype), (message.shape, message.dtype)],
        [resident(value) for value in named.values()],
        aliases={count - 2: 0, count - 1: 1},
        **cost_of(pieces[-1][1]),
    )


def last_step(turn, sources, pieces, schur, products, mask, kepts):
    products = more_products(turn, sources, pieces, schur, products)
    operands = [products, pieces[-1][1], schur, mask] + kepts
    return in_kernel(
        functools.partial(last_kernel, turn, sources),
        [
            (kepts[0].shape, kepts[0].dtype),
            ((len(kepts),) + kepts[0].shape, jnp.bfloat16),
        ],
        [resident(value) for value in operands],
        aliases={4: 0},
        **cost_of(pieces[-1][1]),
    )


def last_kernel(turn, sources, products_ref, other_ref, schur_ref, mask_ref, *refs):
    kepts, kept_ref, message_ref = refs[:-2], refs[-2], refs[-1]
    for panel in range(1, len(kepts)):
        message_ref[panel] = kepts[panel][...].astype(jnp.bfloat16)

    @gated(turn)
    def _():
        origins = sources(lax.axis_index("xy"))[-1][1]
        products = [products_ref[part] for part in range(2)]
        products = part_products(other_ref, origins, schur_ref, products)
        for part, value in enumerate(combined(products)):
            value = kepts[0][part] + mask_ref[...] * value
            kept_ref[part] = value
            message_ref[0, part] = value.astype(jnp.bfloat16)

    @pl.when(lax.axis_index("gz") != turn)
    def _():
        message_ref[0] = kepts[0][...].astype(jnp.bfloat16)


def pick_kernel(sources, which, *refs):
    rows_ref, picked_ref = refs[len(which)], refs[-1]
    origins = sources(lax.axis_index("xy"))
    picked = None
    if len(refs) > len(which) + 2:
        picked = [refs[len(which) + 1][panel] for panel in range(picked_ref.shape[0])]
    for ref, (part, core) in zip(refs, which):
        picked = picks(ref, rows_ref, origins[part][core], picked)
    for panel, value in enumerate(picked):
        picked_ref[panel] = value


def picks(ref, rows_ref, origins, picked):
    _, panel_count, _, side_count, share = ref.shape
    bound = rows_ref.shape[1]
    found = []
    for panel in range(panel_count):
        total = picked[panel] if picked else jnp.zeros((2 * side_count, bound), jnp.float32)
        for place, origin in enumerate(origins):
            rows = origin * share + lax.broadcasted_iota(jnp.int32, (share, bound), 0)
            chosen = jnp.where(rows == rows_ref[pl.ds(panel, 1), :], 1.0, 0.0).astype(jnp.bfloat16)
            field = ref[place, panel].reshape(2 * side_count, share)
            total += jnp.dot(field, chosen, preferred_element_type=jnp.float32)
        found.append(total)
    return found


def inner_kernel(
    sources, picked_ref, last_ref, rows_ref, coupling_ref, inverse_ref, solved_ref, out_ref, inner_ref, sems
):
    contract = (((1,), (1,)), ((), ()))
    origins = sources(lax.axis_index("xy"))[-1][1]
    picked = picks(last_ref, rows_ref, origins, [picked_ref[p] for p in range(picked_ref.shape[0])])
    lifted = [
        combined(
            [
                lax.dot_general(
                    value.astype(jnp.bfloat16),
                    coupling_ref[panel, 0, part],
                    contract,
                    preferred_element_type=jnp.float32,
                )
                for part in range(2)
            ]
        )
        for panel, value in enumerate(picked)
    ]
    copies = []
    for panel, value in enumerate(lifted):
        field = jnp.concatenate(value).astype(jnp.bfloat16)
        back = combined(real_products(field, inverse_ref.at[panel, 0]))
        for part in range(2):
            inner_ref[panel, part] = solved_ref[panel, part] - back[part]
        copies.append(
            pltpu.make_async_copy(inner_ref.at[panel], out_ref.at[panel], sems.at[panel])
        )
        copies[-1].start()
    for copy in copies:
        copy.wait()


def on_device(
    source_inner, source_front, inner_inverse, coupling, schur_inverse, front_rows, link, front_size
):
    peers, groups = lax.axis_size("xy"), lax.axis_size("gz")
    panel_count, _, side_count, share = source_front.shape
    bound = front_rows.shape[1]
    local = source_inner.shape[3]

    tail_rows = 2 * panel_count + 2 * -(-share // bound)
    tail_rows += -tail_rows % 16
    sent_rows = 2 * side_count * panel_count + tail_rows
    taken = [source_inner, inner_inverse, coupling, front_rows, link, source_front]
    row = ((1, share), jnp.float32)
    arriving = ((peers // 4, 1, 1, share), jnp.float32)
    solved, sent, _, inverse_held, coupling_held, rows_held, _, source_held, *scales = in_kernel(
        local_kernel,
        [
            ((panel_count, 2, side_count, local), jnp.float32),
            ((sent_rows, bound), jnp.bfloat16),
        ]
        + [(value.shape, value.dtype) for value in taken]
        + [row] * (3 * panel_count)
        + [arriving] * 4,
        [in_hbm(value) for value in taken + [front_size]],
        specs=[IN_HBM] * (len(taken) + 1),
        scratch=[
            pltpu.SMEM(front_size.shape, jnp.int32),
            pltpu.VMEM((tail_rows, bound), jnp.float32),
            pltpu.SemaphoreType.DMA((len(taken) * panel_count + 1,)),
        ],
    )
    masks, forward_scales = scales[:panel_count], scales[panel_count : 2 * panel_count]
    backward_scales, met = scales[2 * panel_count : 3 * panel_count], scales[3 * panel_count :]

    def push(panel, shards, contrib=None):
        operands = shards + ([] if contrib is None else [contrib])
        return in_kernel(
            functools.partial(push_kernel, panel, panel_count, len(shards)),
            [((2 * side_count, share), jnp.float32)],
            [resident(value) for value in operands],
            moved=2**22,
        )[0]

    shards, contrib, schurs = gathered_within(
        sent, None, lambda mine: push(0, [mine]), [loaded(schur_inverse, sent)]
    )
    shards = [shard for part in shards for shard in part]
    contrib = push(0, shards[1:3], contrib)
    operands = [masks[0], contrib, source_held, shards[3]]
    base, message = in_kernel(
        functools.partial(base_kernel, 0, panel_count),
        [((2, side_count, share), jnp.float32), ((2, side_count, share), jnp.bfloat16)],
        [resident(value) for value in operands],
        moved=2**22,
    )
    bases = [base]
    for panel in range(1, panel_count):
        operands = [resident(value) for value in (masks[panel], source_held, *shards)]
        base, schur = in_kernel(
            functools.partial(later_kernel, panel, panel_count),
            [((2, side_count, share), jnp.float32), (schur_inverse.shape[1:], schur_inverse.dtype)],
            operands + [in_hbm(schur_inverse), message],
            specs=[IN_VMEM] * len(operands) + [IN_HBM, pl.BlockSpec(memory_space=pl.ANY)],
            scratch=[pltpu.SemaphoreType.DMA((8,))],
            moved=2**23,
        )
        bases.append(base)
        schurs.append(schur)
    met[:2] = in_kernel(
        functools.partial(link_kernel, panel_count, side_count),
        [arriving] * 2,
        [resident(value) for value in (met[0], met[1], shards[0], shards[2])],
    )

    kept = [jnp.zeros((2, side_count, share), jnp.float32) for _ in range(panel_count)]
    within, across = sources_by(masks_within(peers)), sources_by(masks_across(peers))
    order = [(turn, panel) for turn in range(groups) for panel in range(panel_count)]
    steps = [(None, 0, True)] + [step + (True,) for step in order[1:]]
    steps += [step + (False,) for step in reversed(order[:-1])]
    for count, (turn, panel, forward) in enumerate(steps):
        if forward and panel == 0 and turn is not None:
            low, by, scales = turn - 1, 1, met[:2]
        elif not forward and panel == panel_count - 1:
            low, by, scales = turn, -1, met[2:]
        else:
            low = None
        sources = within if low is None else across
        first = functools.partial(first_products, turn, sources, schurs[panel])
        if low is not None:
            pieces, products = crossed(message, low, by, scales, first)
        elif count == 0:
            beside = (bases[1:], schurs[1:], met)
            pieces, products, beside = gathered_within(message, None, first, beside)
            bases[1:], schurs[1:], met = beside
        else:
            pieces, products, _ = gathered_within(message, turn, first)
        scale = addend = None
        if forward and panel < panel_count - 1:
            scale, addend = forward_scales[panel + 1], bases[panel + 1]
        elif not forward or turn == groups - 1:
            scale = backward_scales[panel]
        if count == len(steps) - 1:
            kept[0], message = last_step(turn, sources, pieces, schurs[0], products, masks[0], kept)
        else:
            kept[panel], message = sweep_step(
                turn, sources, pieces, schurs[panel], products, kept[panel], message,
                not forward or (panel == 0 and turn is not None),
                mask=masks[panel], scale=scale, addend=addend,
            )

    fronts = jnp.stack(kept)

    def pick(which, parts, *picked):
        return in_kernel(
            functools.partial(pick_kernel, within, which),
            [((panel_count, 2 * side_count, bound), jnp.float32)],
            [resident(value) for value in (*parts, rows_held, *picked)],
            moved=2**22,
        )[0]

    pieces, picked, _ = gathered_within(message, None, lambda mine: pick([(0, 0)], [mine]))
    (_, other), (more, last) = pieces
    picked = pick([(0, 1), (1, 0)], [other, more], picked)
    operands = [picked, last, rows_held, coupling_held, inverse_held, solved]
    inner = pl.pallas_call(
        functools.partial(inner_kernel, within),
        out_shape=jax.ShapeDtypeStruct(solved.shape, jnp.float32),
        in_specs=[IN_VMEM] * len(operands),
        out_specs=IN_HBM,
        scratch_shapes=[
            pltpu.VMEM(solved.shape, jnp.float32),
            pltpu.SemaphoreType.DMA((panel_count,)),
        ],
        compiler_params=pltpu.CompilerParams(vmem_limit_bytes=16 * 2**20),
    )(*[resident(value) for value in operands])
    return inner, fronts


def solution(mesh):
    placed = (
        P("gz", None, None, "xy"),
        P("gz", None, None, "xy"),
        P("gz", "xy", None, None, None),
        P("gz", "xy", None, None, None),
        P("gz", None, None, "xy"),
        P("gz", "xy"),
        P("gz", "xy"),
        P("gz"),
    )
    return jax.shard_map(
        on_device,
        mesh=mesh,
        in_specs=placed,
        out_specs=(P("gz", None, None, "xy"), P("gz", None, None, "xy")),
        check_vma=False,
    )
```

```python
import functools

import jax
import jax.numpy as jnp
from jax import lax
from jax.experimental import pallas as pl
from jax.experimental.pallas import tpu as pltpu
from jax.sharding import PartitionSpec as P

IN_VMEM = pl.BlockSpec(memory_space=pltpu.VMEM)


IN_HBM = pl.BlockSpec(memory_space=pltpu.HBM)
IN_SMEM = pl.BlockSpec(memory_space=pltpu.SMEM)


def resident(array):
    return pltpu.with_memory_space_constraint(array, pltpu.VMEM)


def in_hbm(array):
    return pltpu.with_memory_space_constraint(array, pltpu.HBM)


def swapped(shard, mask, turn=None):
    peers, groups = lax.axis_size("xy"), lax.axis_size("gz")
    pairs = []
    for group in range(groups):
        used = mask if turn is None or (group - turn) % 2 == 0 else 1
        pairs += [(group * peers + peer, group * peers + (peer ^ used)) for peer in range(peers)]
    return lax.ppermute(shard, ("gz", "xy"), pairs)


def masks_within(peers):
    masks = [0] + list(reversed(range(2, peers, 2)))
    return masks[: peers // 4], masks[peers // 4 :]


def in_parts(one, fetched, first, beside=(), join=jnp.stack):
    pieces = [(one, swapped(one, 1))]
    made = first(one)
    fetched, made, beside = lax.optimization_barrier((fetched, made, beside))
    two = join(fetched)
    pieces.append((two, swapped(two, 1)))
    return pieces, made, beside


def gathered_within(message, turn, first, beside=()):
    one, two = [
        [swapped(message, mask, turn) if mask else message for mask in part]
        for part in masks_within(lax.axis_size("xy"))
    ]
    return in_parts(jnp.stack(one), two, first, beside)


def sources_by(parts):
    def sources(me):
        found = []
        for masks in parts:
            mine = [me ^ mask for mask in masks]
            found.append((mine, [peer ^ 1 for peer in mine]))
        return found

    return sources


def masks_across(peers):
    masks = list(reversed(range(0, peers, 2)))
    return masks[: peers // 4], masks[peers // 4 :]


def crossed(message, low, by, scales, first):
    peers, groups = lax.axis_size("xy"), lax.axis_size("gz")

    def across(mask):
        pairs = []
        for group in range(groups):
            lower = group if (group - low) % 2 == 0 else group - 1
            joined = 0 <= lower and lower + 1 < groups
            for peer in range(peers):
                if mask == 0:
                    place = (2 * lower + 1 - group) * peers + peer if joined else group * peers + (peer ^ 1)
                elif joined and group == (lower if by > 0 else lower + 1):
                    place = (group + by) * peers + (peer ^ mask)
                else:
                    continue
                pairs.append((group * peers + peer, place))
        return lax.ppermute(message, ("gz", "xy"), pairs)

    def scaled(part, scale):
        return (scale * jnp.stack(part).astype(jnp.float32)).astype(jnp.bfloat16)

    one, two = [[across(mask) for mask in part] for part in masks_across(peers)]
    join = functools.partial(scaled, scale=scales[1])
    return in_parts(scaled(one, scales[0]), two, first, join=join)[:2]


def gated(turn):
    def wrap(body):
        if turn is None:
            body()
        else:
            pl.when(lax.axis_index("gz") == turn)(body)

    return wrap


def in_kernel(body, outs, operands, aliases=None, specs=None, scratch=(), flops=0, moved=0):
    return pl.pallas_call(
        body,
        out_shape=tuple(pltpu.VMEM(shape, dtype) for shape, dtype in outs),
        in_specs=specs or [IN_VMEM] * len(operands),
        out_specs=(IN_VMEM,) * len(outs),
        scratch_shapes=scratch,
        input_output_aliases=aliases or {},
        compiler_params=pltpu.CompilerParams(vmem_limit_bytes=16 * 2**20),
        cost_estimate=pl.CostEstimate(flops=flops, bytes_accessed=moved, transcendentals=0),
    )(*operands)


def real_products(field, matrix):
    return [
        jnp.dot(field, matrix[part], preferred_element_type=jnp.float32) for part in range(2)
    ]


def combined(products):
    first, second = products
    count = first.shape[0] // 2
    return first[:count] - second[count:], second[:count] + first[count:]


def panel_copies(panel, schur_ref, out_ref, sems):
    chunks = sems.shape[0] // 2
    rows = schur_ref.shape[2] // chunks
    copies = []
    for part in range(2):
        for chunk in range(chunks):
            span = pl.ds(chunk * rows, rows)
            copies.append(
                pltpu.make_async_copy(
                    schur_ref.at[panel, part, span, :],
                    out_ref.at[part, span, :],
                    sems.at[part * chunks + chunk],
                )
            )
    for copy in copies:
        copy.start()
    return copies


def load_kernel(schur_ref, after_ref, out_ref, sems):
    del after_ref
    for copy in panel_copies(0, schur_ref, out_ref, sems):
        copy.wait()


def loaded(schur, after):
    return in_kernel(
        load_kernel,
        [(schur.shape[1:], schur.dtype)],
        [in_hbm(schur), after],
        specs=[IN_HBM, pl.BlockSpec(memory_space=pl.ANY)],
        scratch=[pltpu.SemaphoreType.DMA((8,))],
        moved=schur.dtype.itemsize * schur[0].size,
    )[0]


def local_kernel(*refs):
    operands, size_in, (solved_ref, sent_ref), held = refs[:6], refs[6], refs[7:9], refs[9:15]
    rows_out, met, (sizes, tail_ref, sems) = refs[15:-7], refs[-7:-3], refs[-3:]
    source_ref, inverse_ref, coupling_ref, rows_ref, link_ref, _ = held
    panel_count, _, side_count, _ = source_ref.shape
    bound, share = sent_ref.shape[1], link_ref.shape[1]
    ends = []
    for panel in range(panel_count):
        ends.append((operands[0].at[panel], held[0].at[panel]))
        for operand, place in zip(operands[1:3], held[1:3]):
            for part in range(2):
                ends.append((operand.at[panel, 0, part], place.at[panel, 0, part]))
    ends += list(zip(operands[3:], held[3:])) + [(size_in, sizes)]
    copies = [
        pltpu.make_async_copy(operand, place, sems.at[index])
        for index, (operand, place) in enumerate(ends)
    ]
    for copy in copies:
        copy.start()
    for panel in range(panel_count):
        for copy in copies[5 * panel : 5 * panel + 3]:
            copy.wait()
        field = source_ref[panel].astype(jnp.bfloat16).reshape(2 * side_count, -1)
        solved = combined(real_products(field, inverse_ref.at[panel, 0]))
        for part in range(2):
            solved_ref[panel, part] = solved[part]
        field = jnp.concatenate(solved).astype(jnp.bfloat16)
        for copy in copies[5 * panel + 3 : 5 * panel + 5]:
            copy.wait()
        pushed = combined(real_products(field, coupling_ref.at[panel, 0]))
        for part in range(2):
            start = (2 * panel + part) * side_count
            sent_ref[pl.ds(start, side_count), :] = pushed[part].astype(jnp.bfloat16)
    for copy in copies[5 * panel_count :]:
        copy.wait()
    tail_ref[...] = jnp.zeros(tail_ref.shape, jnp.float32)
    for panel in range(panel_count):
        rows = rows_ref[pl.ds(panel, 1), :]
        tail_ref[pl.ds(panel, 1), :] = (rows >> 8).astype(jnp.float32)
        tail_ref[pl.ds(panel_count + panel, 1), :] = (rows & 255).astype(jnp.float32)
    row = 2 * panel_count
    for start in range(0, share, bound):
        width = min(bound, share - start)
        link = link_ref[pl.ds(0, 1), pl.ds(start, width)]
        high = link.astype(jnp.bfloat16).astype(jnp.float32)
        tail_ref[pl.ds(row, 1), pl.ds(0, width)] = high
        tail_ref[pl.ds(row + 1, 1), pl.ds(0, width)] = link - high
        row += 2
    first = 2 * side_count * panel_count
    sent_ref[pl.ds(first, tail_ref.shape[0]), :] = tail_ref[...].astype(jnp.bfloat16)
    me = lax.axis_index("xy")
    masks = [live(sizes, panel, me * share, share) for panel in range(panel_count)]
    for panel in range(panel_count):
        link = link_ref[pl.ds(panel, 1), :]
        rows_out[panel][...] = masks[panel]
        rows_out[panel_count + panel][...] = masks[panel] * link
        rows_out[2 * panel_count + panel][...] = link * masks[panel - 1] if panel else link
    for half, part in enumerate(masks_across(4 * met[0].shape[0])):
        for index, mask in enumerate(part):
            start = (me ^ mask) * share
            met[half][index, 0] = live(sizes, 0, start, share)
            met[2 + half][index, 0] = live(sizes, panel_count - 1, start, share)


def tail_of(ref, place, first):
    return ref[place, pl.ds(first, ref.shape[1] - first), :].astype(jnp.float32)


def live(size_ref, panel, start, share):
    rows = start + lax.broadcasted_iota(jnp.int32, (1, share), 1)
    return jnp.where(rows < size_ref[panel], 1.0, 0.0)


def pushed_up(panel, panel_count, count, share, refs, contrib):
    bound = refs[0].shape[2]
    own_rows = lax.axis_index("xy") * share + lax.broadcasted_iota(jnp.int32, (share, bound), 0)
    contract = (((1,), (1,)), ((), ()))
    for ref in refs:
        for place in range(ref.shape[0]):
            values = ref[place, pl.ds(count * panel, count), :]
            tail = tail_of(ref, place, count * panel_count)
            high = tail[panel : panel + 1]
            low = tail[panel_count + panel : panel_count + panel + 1]
            places = (256.0 * high + low).astype(jnp.int32)
            hits = jnp.where(own_rows == places, 1.0, 0.0).astype(jnp.bfloat16)
            contrib += lax.dot_general(values, hits, contract, preferred_element_type=jnp.float32)
    return contrib


def push_kernel(panel, panel_count, parts, *refs):
    contrib_ref = refs[-1]
    count, share = contrib_ref.shape
    contrib = refs[parts][...] if len(refs) > parts + 1 else jnp.zeros((count, share), jnp.float32)
    contrib_ref[...] = pushed_up(panel, panel_count, count, share, refs[:parts], contrib)


def base_kernel(panel, panel_count, mask_ref, contrib_ref, source_ref, *refs):
    refs, base_ref, message_ref = refs[:-2], refs[-2], refs[-1]
    _, side_count, share = base_ref.shape
    count = 2 * side_count
    contrib = pushed_up(panel, panel_count, count, share, refs, contrib_ref[...])
    for part in range(2):
        rows = slice(part * side_count, (part + 1) * side_count)
        base = mask_ref[...] * (source_ref[panel, part] - contrib[rows])
        base_ref[part] = base
        message_ref[part] = base.astype(jnp.bfloat16)


def later_kernel(panel, panel_count, mask_ref, source_ref, *refs):
    shards, schur_ref, base_ref, out_ref, sems = refs[:4], refs[4], refs[6], refs[7], refs[8]
    copies = panel_copies(panel, schur_ref, out_ref, sems)
    _, side_count, share = base_ref.shape
    count = 2 * side_count
    zeros = jnp.zeros((count, share), jnp.float32)
    contrib = pushed_up(panel, panel_count, count, share, shards, zeros)
    for part in range(2):
        rows = slice(part * side_count, (part + 1) * side_count)
        base_ref[part] = mask_ref[...] * (source_ref[panel, part] - contrib[rows])
    for copy in copies:
        copy.wait()


def link_kernel(panel_count, side_count, one_mask, two_mask, one_ref, two_ref, one_out, two_out):
    share, bound = one_out.shape[3], one_ref.shape[2]
    peers = 4 * one_out.shape[0]
    tails = {}
    for ref, part in zip((one_ref, two_ref), masks_within(peers)):
        for index, mask in enumerate(part):
            tails[mask] = tail_of(ref, index, 2 * side_count * panel_count)
    for mask_ref, out, part in zip((one_mask, two_mask), (one_out, two_out), masks_across(peers)):
        for index, mask in enumerate(part):
            for piece, place in enumerate(range(0, share, bound)):
                columns = pl.ds(place, min(bound, share - place))
                row = 2 * (panel_count + piece)
                link = tails[mask][row : row + 1] + tails[mask][row + 1 : row + 2]
                out[index, 0, :, columns] = mask_ref[index, 0, :, columns] * link[:, : columns.size]


def part_products(ref, origins, schur_ref, products):
    side_count, share = ref.shape[2:]
    for place, origin in enumerate(origins):
        rows = pl.ds(pl.multiple_of(origin * share, share), share)
        field = ref[place].reshape(2 * side_count, share)
        terms = real_products(field, schur_ref.at[:, rows, :])
        products = terms if products is None else [a + b for a, b in zip(products, terms)]
    return products


def products_kernel(turn, sources, which, *refs):
    schur_ref, products_ref = refs[len(which)], refs[-1]

    @gated(turn)
    def _():
        origins = sources(lax.axis_index("xy"))
        products = None
        if len(refs) > len(which) + 2:
            products = [refs[len(which) + 1][part] for part in range(2)]
        for ref, (part, core) in zip(refs, which):
            products = part_products(ref, origins[part][core], schur_ref, products)
        for part in range(2):
            products_ref[part] = products[part]


def late_kernel(turn, sources, names, *refs):
    named = dict(zip(names, refs))
    kept_ref, message_ref = refs[-2:]

    @gated(turn)
    def _():
        origins = sources(lax.axis_index("xy"))[-1][1]
        products = [named["products"][part] for part in range(2)]
        products = part_products(named["other"], origins, named["schur"], products)
        for part, value in enumerate(combined(products)):
            value = named["mask"][...] * value
            if "kept" in named:
                value = named["kept"][part] + value
            kept_ref[part] = value
            if "scale" in named:
                value = named["scale"][...] * value
            if "addend" in named:
                value = named["addend"][part] + value
            message_ref[part] = value.astype(jnp.bfloat16)


def cost_of(mine):
    _, _, side_count, share = mine.shape
    return {
        "flops": 8 * side_count * share * share * mine.shape[0],
        "moved": 4 * share * share * mine.shape[0],
    }


def products_of(turn, sources, which, parts, schur, products=None):
    side_count, share = parts[0].shape[2:]
    operands = [*parts, schur] + ([] if products is None else [products])
    return in_kernel(
        functools.partial(products_kernel, turn, sources, which),
        [((2, 2 * side_count, share), jnp.float32)],
        [resident(value) for value in operands],
        **cost_of(parts[0]),
    )[0]


def first_products(turn, sources, schur, mine):
    return products_of(turn, sources, [(0, 0)], [mine], schur)


def more_products(turn, sources, pieces, schur, products):
    (_, other), (more, _) = pieces
    return products_of(turn, sources, [(0, 1), (1, 0)], [other, more], schur, products)


def sweep_step(turn, sources, pieces, schur, products, kept, message, adds, **others):
    products = more_products(turn, sources, pieces, schur, products)
    named = {"products": products, "other": pieces[-1][1], "schur": schur}
    named.update({name: value for name, value in others.items() if value is not None})
    named["kept" if adds else "old"], named["message"] = kept, message
    count = len(named)
    return in_kernel(
        functools.partial(late_kernel, turn, sources, list(named)),
        [(kept.shape, kept.dtype), (message.shape, message.dtype)],
        [resident(value) for value in named.values()],
        aliases={count - 2: 0, count - 1: 1},
        **cost_of(pieces[-1][1]),
    )


def last_step(turn, sources, pieces, schur, products, mask, kepts):
    products = more_products(turn, sources, pieces, schur, products)
    operands = [products, pieces[-1][1], schur, mask] + kepts
    return in_kernel(
        functools.partial(last_kernel, turn, sources),
        [
            (kepts[0].shape, kepts[0].dtype),
            ((len(kepts),) + kepts[0].shape, jnp.bfloat16),
        ],
        [resident(value) for value in operands],
        aliases={4: 0},
        **cost_of(pieces[-1][1]),
    )


def last_kernel(turn, sources, products_ref, other_ref, schur_ref, mask_ref, *refs):
    kepts, kept_ref, message_ref = refs[:-2], refs[-2], refs[-1]
    for panel in range(1, len(kepts)):
        message_ref[panel] = kepts[panel][...].astype(jnp.bfloat16)

    @gated(turn)
    def _():
        origins = sources(lax.axis_index("xy"))[-1][1]
        products = [products_ref[part] for part in range(2)]
        products = part_products(other_ref, origins, schur_ref, products)
        for part, value in enumerate(combined(products)):
            value = kepts[0][part] + mask_ref[...] * value
            kept_ref[part] = value
            message_ref[0, part] = value.astype(jnp.bfloat16)

    @pl.when(lax.axis_index("gz") != turn)
    def _():
        message_ref[0] = kepts[0][...].astype(jnp.bfloat16)


def pick_kernel(sources, which, *refs):
    rows_ref, picked_ref = refs[len(which)], refs[-1]
    origins = sources(lax.axis_index("xy"))
    picked = None
    if len(refs) > len(which) + 2:
        picked = [refs[len(which) + 1][panel] for panel in range(picked_ref.shape[0])]
    for ref, (part, core) in zip(refs, which):
        picked = picks(ref, rows_ref, origins[part][core], picked)
    for panel, value in enumerate(picked):
        picked_ref[panel] = value


def picks(ref, rows_ref, origins, picked):
    _, panel_count, _, side_count, share = ref.shape
    bound = rows_ref.shape[1]
    found = []
    for panel in range(panel_count):
        total = picked[panel] if picked else jnp.zeros((2 * side_count, bound), jnp.float32)
        for place, origin in enumerate(origins):
            rows = origin * share + lax.broadcasted_iota(jnp.int32, (share, bound), 0)
            chosen = jnp.where(rows == rows_ref[pl.ds(panel, 1), :], 1.0, 0.0).astype(jnp.bfloat16)
            field = ref[place, panel].reshape(2 * side_count, share)
            total += jnp.dot(field, chosen, preferred_element_type=jnp.float32)
        found.append(total)
    return found


def first_pick_kernel(sources, mine_ref, rows_ref, picked_ref, chosen_ref):
    (origins, _), (_, lasts) = sources(lax.axis_index("xy"))
    for panel, value in enumerate(picks(mine_ref, rows_ref, origins, None)):
        picked_ref[panel] = value
    panel_count, _, share, bound = chosen_ref.shape
    for panel in range(panel_count):
        for index, origin in enumerate(lasts):
            rows = origin * share + lax.broadcasted_iota(jnp.int32, (share, bound), 0)
            hits = jnp.where(rows == rows_ref[pl.ds(panel, 1), :], 1.0, 0.0)
            chosen_ref[panel, index] = hits.astype(jnp.bfloat16)


def inner_kernel(
    picked_ref, last_ref, chosen_ref, coupling_ref, inverse_ref, solved_ref, out_ref, inner_ref, sems
):
    contract = (((1,), (1,)), ((), ()))
    _, panel_count, _, side_count, share = last_ref.shape
    picked = []
    for panel in range(panel_count):
        total = picked_ref[panel]
        for place in range(last_ref.shape[0]):
            field = last_ref[place, panel].reshape(2 * side_count, share)
            total += jnp.dot(field, chosen_ref[panel, place], preferred_element_type=jnp.float32)
        picked.append(total)
    lifted = [
        combined(
            [
                lax.dot_general(
                    value.astype(jnp.bfloat16),
                    coupling_ref[panel, 0, part],
                    contract,
                    preferred_element_type=jnp.float32,
                )
                for part in range(2)
            ]
        )
        for panel, value in enumerate(picked)
    ]
    copies = []
    for panel, value in enumerate(lifted):
        field = jnp.concatenate(value).astype(jnp.bfloat16)
        back = combined(real_products(field, inverse_ref.at[panel, 0]))
        for part in range(2):
            inner_ref[panel, part] = solved_ref[panel, part] - back[part]
        copies.append(
            pltpu.make_async_copy(inner_ref.at[panel], out_ref.at[panel], sems.at[panel])
        )
        copies[-1].start()
    for copy in copies:
        copy.wait()


def on_device(
    source_inner, source_front, inner_inverse, coupling, schur_inverse, front_rows, link, front_size
):
    peers, groups = lax.axis_size("xy"), lax.axis_size("gz")
    panel_count, _, side_count, share = source_front.shape
    bound = front_rows.shape[1]
    local = source_inner.shape[3]

    tail_rows = 2 * panel_count + 2 * -(-share // bound)
    tail_rows += -tail_rows % 16
    sent_rows = 2 * side_count * panel_count + tail_rows
    taken = [source_inner, inner_inverse, coupling, front_rows, link, source_front]
    row = ((1, share), jnp.float32)
    arriving = ((peers // 4, 1, 1, share), jnp.float32)
    solved, sent, _, inverse_held, coupling_held, rows_held, _, source_held, *scales = in_kernel(
        local_kernel,
        [
            ((panel_count, 2, side_count, local), jnp.float32),
            ((sent_rows, bound), jnp.bfloat16),
        ]
        + [(value.shape, value.dtype) for value in taken]
        + [row] * (3 * panel_count)
        + [arriving] * 4,
        [in_hbm(value) for value in taken + [front_size]],
        specs=[IN_HBM] * (len(taken) + 1),
        scratch=[
            pltpu.SMEM(front_size.shape, jnp.int32),
            pltpu.VMEM((tail_rows, bound), jnp.float32),
            pltpu.SemaphoreType.DMA((5 * panel_count + 4,)),
        ],
    )
    masks, forward_scales = scales[:panel_count], scales[panel_count : 2 * panel_count]
    backward_scales, met = scales[2 * panel_count : 3 * panel_count], scales[3 * panel_count :]

    def push(panel, shards, contrib=None):
        operands = shards + ([] if contrib is None else [contrib])
        return in_kernel(
            functools.partial(push_kernel, panel, panel_count, len(shards)),
            [((2 * side_count, share), jnp.float32)],
            [resident(value) for value in operands],
        )[0]

    shards, contrib, schurs = gathered_within(
        sent, None, lambda mine: push(0, [mine]), [loaded(schur_inverse, sent)]
    )
    shards = [shard for part in shards for shard in part]
    contrib = push(0, shards[1:3], contrib)
    operands = [masks[0], contrib, source_held, shards[3]]
    base, message = in_kernel(
        functools.partial(base_kernel, 0, panel_count),
        [((2, side_count, share), jnp.float32), ((2, side_count, share), jnp.bfloat16)],
        [resident(value) for value in operands],
        moved=2**22,
    )
    bases = [base]
    for panel in range(1, panel_count):
        operands = [resident(value) for value in (masks[panel], source_held, *shards)]
        base, schur = in_kernel(
            functools.partial(later_kernel, panel, panel_count),
            [((2, side_count, share), jnp.float32), (schur_inverse.shape[1:], schur_inverse.dtype)],
            operands + [in_hbm(schur_inverse), message],
            specs=[IN_VMEM] * len(operands) + [IN_HBM, pl.BlockSpec(memory_space=pl.ANY)],
            scratch=[pltpu.SemaphoreType.DMA((8,))],
            moved=2**23,
        )
        bases.append(base)
        schurs.append(schur)
    met[:2] = in_kernel(
        functools.partial(link_kernel, panel_count, side_count),
        [arriving] * 2,
        [resident(value) for value in (met[0], met[1], shards[0], shards[2])],
    )

    kept = [jnp.zeros((2, side_count, share), jnp.float32) for _ in range(panel_count)]
    within, across = sources_by(masks_within(peers)), sources_by(masks_across(peers))
    order = [(turn, panel) for turn in range(groups) for panel in range(panel_count)]
    steps = [(None, 0, True)] + [step + (True,) for step in order[1:]]
    steps += [step + (False,) for step in reversed(order[:-1])]
    for count, (turn, panel, forward) in enumerate(steps):
        if forward and panel == 0 and turn is not None:
            low, by, scales = turn - 1, 1, met[:2]
        elif not forward and panel == panel_count - 1:
            low, by, scales = turn, -1, met[2:]
        else:
            low = None
        sources = within if low is None else across
        first = functools.partial(first_products, turn, sources, schurs[panel])
        if low is not None:
            pieces, products = crossed(message, low, by, scales, first)
        elif count == 0:
            beside = (bases[1:], schurs[1:], met)
            pieces, products, beside = gathered_within(message, None, first, beside)
            bases[1:], schurs[1:], met = beside
        else:
            pieces, products, _ = gathered_within(message, turn, first)
        scale = addend = None
        if forward and panel < panel_count - 1:
            scale, addend = forward_scales[panel + 1], bases[panel + 1]
        elif not forward or turn == groups - 1:
            scale = backward_scales[panel]
        if count == len(steps) - 1:
            kept[0], message = last_step(turn, sources, pieces, schurs[0], products, masks[0], kept)
        else:
            kept[panel], message = sweep_step(
                turn, sources, pieces, schurs[panel], products, kept[panel], message,
                not forward or (panel == 0 and turn is not None),
                mask=masks[panel], scale=scale, addend=addend,
            )

    fronts = jnp.stack(kept)

    def pick(which, parts, *picked):
        return in_kernel(
            functools.partial(pick_kernel, within, which),
            [((panel_count, 2 * side_count, bound), jnp.float32)],
            [resident(value) for value in (*parts, rows_held, *picked)],
            moved=2**22,
        )[0]

    def first_pick(mine):
        return in_kernel(
            functools.partial(first_pick_kernel, within),
            [
                ((panel_count, 2 * side_count, bound), jnp.float32),
                ((panel_count, peers // 2 - mine.shape[0], share, bound), jnp.bfloat16),
            ],
            [resident(mine), resident(rows_held)],
            moved=2**22,
        )

    pieces, (picked, chosen), _ = gathered_within(message, None, first_pick)
    (_, other), (more, last) = pieces
    picked = pick([(0, 1), (1, 0)], [other, more], picked)
    operands = [picked, last, chosen, coupling_held, inverse_held, solved]
    inner = pl.pallas_call(
        inner_kernel,
        out_shape=jax.ShapeDtypeStruct(solved.shape, jnp.float32),
        in_specs=[IN_VMEM] * len(operands),
        out_specs=IN_HBM,
        scratch_shapes=[
            pltpu.VMEM(solved.shape, jnp.float32),
            pltpu.SemaphoreType.DMA((panel_count,)),
        ],
        compiler_params=pltpu.CompilerParams(vmem_limit_bytes=16 * 2**20),
    )(*[resident(value) for value in operands])
    return inner, fronts


def solution(mesh):
    placed = (
        P("gz", None, None, "xy"),
        P("gz", None, None, "xy"),
        P("gz", "xy", None, None, None),
        P("gz", "xy", None, None, None),
        P("gz", None, None, "xy"),
        P("gz", "xy"),
        P("gz", "xy"),
        P("gz"),
    )
    return jax.shard_map(
        on_device,
        mesh=mesh,
        in_specs=placed,
        out_specs=(P("gz", None, None, "xy"), P("gz", None, None, "xy")),
        check_vma=False,
    )
```

```python
import functools

import jax
import jax.numpy as jnp
from jax import lax
from jax.experimental import pallas as pl
from jax.experimental.pallas import tpu as pltpu
from jax.sharding import PartitionSpec as P

IN_VMEM = pl.BlockSpec(memory_space=pltpu.VMEM)


IN_HBM = pl.BlockSpec(memory_space=pltpu.HBM)
IN_SMEM = pl.BlockSpec(memory_space=pltpu.SMEM)


def resident(array):
    return pltpu.with_memory_space_constraint(array, pltpu.VMEM)


def in_hbm(array):
    return pltpu.with_memory_space_constraint(array, pltpu.HBM)


def swapped(shard, mask, turn=None):
    peers, groups = lax.axis_size("xy"), lax.axis_size("gz")
    pairs = []
    for group in range(groups):
        used = mask if turn is None or (group - turn) % 2 == 0 else 1
        pairs += [(group * peers + peer, group * peers + (peer ^ used)) for peer in range(peers)]
    return lax.ppermute(shard, ("gz", "xy"), pairs)


def masks_within(peers):
    masks = [0] + list(reversed(range(2, peers, 2)))
    return masks[: peers // 4], masks[peers // 4 :]


def in_parts(one, fetched, first, beside=(), join=jnp.stack):
    pieces = [(one, swapped(one, 1))]
    made = first(one)
    fetched, made, beside = lax.optimization_barrier((fetched, made, beside))
    two = join(fetched)
    pieces.append((two, swapped(two, 1)))
    return pieces, made, beside


def gathered_within(message, turn, first, beside=()):
    one, two = [
        [swapped(message, mask, turn) if mask else message for mask in part]
        for part in masks_within(lax.axis_size("xy"))
    ]
    return in_parts(jnp.stack(one), two, first, beside)


def sources_by(parts):
    def sources(me):
        found = []
        for masks in parts:
            mine = [me ^ mask for mask in masks]
            found.append((mine, [peer ^ 1 for peer in mine]))
        return found

    return sources


def masks_across(peers):
    masks = list(reversed(range(0, peers, 2)))
    return masks[: peers // 4], masks[peers // 4 :]


def crossed(message, low, by, scales, first):
    peers, groups = lax.axis_size("xy"), lax.axis_size("gz")

    def across(mask):
        pairs = []
        for group in range(groups):
            lower = group if (group - low) % 2 == 0 else group - 1
            joined = 0 <= lower and lower + 1 < groups
            for peer in range(peers):
                if mask == 0:
                    place = (2 * lower + 1 - group) * peers + peer if joined else group * peers + (peer ^ 1)
                elif joined and group == (lower if by > 0 else lower + 1):
                    place = (group + by) * peers + (peer ^ mask)
                else:
                    continue
                pairs.append((group * peers + peer, place))
        return lax.ppermute(message, ("gz", "xy"), pairs)

    def scaled(part, scale):
        return (scale * jnp.stack(part).astype(jnp.float32)).astype(jnp.bfloat16)

    one, two = [[across(mask) for mask in part] for part in masks_across(peers)]
    join = functools.partial(scaled, scale=scales[1])
    return in_parts(scaled(one, scales[0]), two, first, join=join)[:2]


def gated(turn):
    def wrap(body):
        if turn is None:
            body()
        else:
            pl.when(lax.axis_index("gz") == turn)(body)

    return wrap


def in_kernel(body, outs, operands, aliases=None, specs=None, scratch=(), flops=0, moved=0):
    return pl.pallas_call(
        body,
        out_shape=tuple(pltpu.VMEM(shape, dtype) for shape, dtype in outs),
        in_specs=specs or [IN_VMEM] * len(operands),
        out_specs=(IN_VMEM,) * len(outs),
        scratch_shapes=scratch,
        input_output_aliases=aliases or {},
        compiler_params=pltpu.CompilerParams(vmem_limit_bytes=16 * 2**20),
        cost_estimate=pl.CostEstimate(flops=flops, bytes_accessed=moved, transcendentals=0),
    )(*operands)


def real_products(field, matrix):
    return [
        jnp.dot(field, matrix[part], preferred_element_type=jnp.float32) for part in range(2)
    ]


def combined(products):
    first, second = products
    count = first.shape[0] // 2
    return first[:count] - second[count:], second[:count] + first[count:]


def panel_copies(panel, schur_ref, out_ref, sems):
    chunks = sems.shape[0] // 2
    rows = schur_ref.shape[2] // chunks
    copies = []
    for part in range(2):
        for chunk in range(chunks):
            span = pl.ds(chunk * rows, rows)
            copies.append(
                pltpu.make_async_copy(
                    schur_ref.at[panel, part, span, :],
                    out_ref.at[part, span, :],
                    sems.at[part * chunks + chunk],
                )
            )
    for copy in copies:
        copy.start()
    return copies


def load_kernel(schur_ref, after_ref, out_ref, sems):
    del after_ref
    for copy in panel_copies(0, schur_ref, out_ref, sems):
        copy.wait()


def loaded(schur, after):
    return in_kernel(
        load_kernel,
        [(schur.shape[1:], schur.dtype)],
        [in_hbm(schur), after],
        specs=[IN_HBM, pl.BlockSpec(memory_space=pl.ANY)],
        scratch=[pltpu.SemaphoreType.DMA((8,))],
        moved=schur.dtype.itemsize * schur[0].size,
    )[0]


def local_kernel(*refs):
    operands, size_in, (solved_ref, sent_ref), held = refs[:6], refs[6], refs[7:9], refs[9:15]
    rows_out, met, (sizes, tail_ref, sems) = refs[15:-7], refs[-7:-3], refs[-3:]
    source_ref, inverse_ref, coupling_ref, rows_ref, link_ref, _ = held
    panel_count, _, side_count, _ = source_ref.shape
    bound, share = sent_ref.shape[1], link_ref.shape[1]
    ends = []
    for panel in range(panel_count):
        ends.append((operands[0].at[panel], held[0].at[panel]))
        for operand, place in zip(operands[1:3], held[1:3]):
            for part in range(2):
                ends.append((operand.at[panel, 0, part], place.at[panel, 0, part]))
    ends += list(zip(operands[3:], held[3:])) + [(size_in, sizes)]
    copies = [
        pltpu.make_async_copy(operand, place, sems.at[index])
        for index, (operand, place) in enumerate(ends)
    ]
    for copy in copies:
        copy.start()
    for panel in range(panel_count):
        for copy in copies[5 * panel : 5 * panel + 3]:
            copy.wait()
        field = source_ref[panel].astype(jnp.bfloat16).reshape(2 * side_count, -1)
        solved = combined(real_products(field, inverse_ref.at[panel, 0]))
        for part in range(2):
            solved_ref[panel, part] = solved[part]
        field = jnp.concatenate(solved).astype(jnp.bfloat16)
        for copy in copies[5 * panel + 3 : 5 * panel + 5]:
            copy.wait()
        pushed = combined(real_products(field, coupling_ref.at[panel, 0]))
        for part in range(2):
            start = (2 * panel + part) * side_count
            sent_ref[pl.ds(start, side_count), :] = pushed[part].astype(jnp.bfloat16)
    for copy in copies[5 * panel_count :]:
        copy.wait()
    tail_ref[...] = jnp.zeros(tail_ref.shape, jnp.float32)
    for panel in range(panel_count):
        rows = rows_ref[pl.ds(panel, 1), :]
        tail_ref[pl.ds(panel, 1), :] = (rows >> 8).astype(jnp.float32)
        tail_ref[pl.ds(panel_count + panel, 1), :] = (rows & 255).astype(jnp.float32)
    row = 2 * panel_count
    for start in range(0, share, bound):
        width = min(bound, share - start)
        link = link_ref[pl.ds(0, 1), pl.ds(start, width)]
        high = link.astype(jnp.bfloat16).astype(jnp.float32)
        tail_ref[pl.ds(row, 1), pl.ds(0, width)] = high
        tail_ref[pl.ds(row + 1, 1), pl.ds(0, width)] = link - high
        row += 2
    first = 2 * side_count * panel_count
    sent_ref[pl.ds(first, tail_ref.shape[0]), :] = tail_ref[...].astype(jnp.bfloat16)
    me = lax.axis_index("xy")
    masks = [live(sizes, panel, me * share, share) for panel in range(panel_count)]
    for panel in range(panel_count):
        link = link_ref[pl.ds(panel, 1), :]
        rows_out[panel][...] = masks[panel]
        rows_out[panel_count + panel][...] = masks[panel] * link
        rows_out[2 * panel_count + panel][...] = link * masks[panel - 1] if panel else link
    for half, part in enumerate(masks_across(4 * met[0].shape[0])):
        for index, mask in enumerate(part):
            start = (me ^ mask) * share
            met[half][index, 0] = live(sizes, 0, start, share)
            met[2 + half][index, 0] = live(sizes, panel_count - 1, start, share)


def tail_of(ref, place, first):
    return ref[place, pl.ds(first, ref.shape[1] - first), :].astype(jnp.float32)


def live(size_ref, panel, start, share):
    rows = start + lax.broadcasted_iota(jnp.int32, (1, share), 1)
    return jnp.where(rows < size_ref[panel], 1.0, 0.0)


def pushed_up(panel, panel_count, count, share, refs, contrib):
    bound = refs[0].shape[2]
    own_rows = lax.axis_index("xy") * share + lax.broadcasted_iota(jnp.int32, (share, bound), 0)
    contract = (((1,), (1,)), ((), ()))
    for ref in refs:
        for place in range(ref.shape[0]):
            values = ref[place, pl.ds(count * panel, count), :]
            tail = tail_of(ref, place, count * panel_count)
            high = tail[panel : panel + 1]
            low = tail[panel_count + panel : panel_count + panel + 1]
            places = (256.0 * high + low).astype(jnp.int32)
            hits = jnp.where(own_rows == places, 1.0, 0.0).astype(jnp.bfloat16)
            contrib += lax.dot_general(values, hits, contract, preferred_element_type=jnp.float32)
    return contrib


def push_kernel(panel, panel_count, parts, *refs):
    contrib_ref = refs[-1]
    count, share = contrib_ref.shape
    contrib = refs[parts][...] if len(refs) > parts + 1 else jnp.zeros((count, share), jnp.float32)
    contrib_ref[...] = pushed_up(panel, panel_count, count, share, refs[:parts], contrib)


def base_kernel(panel, panel_count, mask_ref, contrib_ref, source_ref, *refs):
    refs, base_ref, message_ref = refs[:-2], refs[-2], refs[-1]
    _, side_count, share = base_ref.shape
    count = 2 * side_count
    contrib = pushed_up(panel, panel_count, count, share, refs, contrib_ref[...])
    for part in range(2):
        rows = slice(part * side_count, (part + 1) * side_count)
        base = mask_ref[...] * (source_ref[panel, part] - contrib[rows])
        base_ref[part] = base
        message_ref[part] = base.astype(jnp.bfloat16)


def later_kernel(panel, panel_count, mask_ref, source_ref, *refs):
    shards, schur_ref, base_ref, out_ref, sems = refs[:4], refs[4], refs[6], refs[7], refs[8]
    copies = panel_copies(panel, schur_ref, out_ref, sems)
    _, side_count, share = base_ref.shape
    count = 2 * side_count
    zeros = jnp.zeros((count, share), jnp.float32)
    contrib = pushed_up(panel, panel_count, count, share, shards, zeros)
    for part in range(2):
        rows = slice(part * side_count, (part + 1) * side_count)
        base_ref[part] = mask_ref[...] * (source_ref[panel, part] - contrib[rows])
    for copy in copies:
        copy.wait()


def link_kernel(panel_count, side_count, one_mask, two_mask, one_ref, two_ref, one_out, two_out):
    share, bound = one_out.shape[3], one_ref.shape[2]
    peers = 4 * one_out.shape[0]
    tails = {}
    for ref, part in zip((one_ref, two_ref), masks_within(peers)):
        for index, mask in enumerate(part):
            tails[mask] = tail_of(ref, index, 2 * side_count * panel_count)
    for mask_ref, out, part in zip((one_mask, two_mask), (one_out, two_out), masks_across(peers)):
        for index, mask in enumerate(part):
            for piece, place in enumerate(range(0, share, bound)):
                columns = pl.ds(place, min(bound, share - place))
                row = 2 * (panel_count + piece)
                link = tails[mask][row : row + 1] + tails[mask][row + 1 : row + 2]
                out[index, 0, :, columns] = mask_ref[index, 0, :, columns] * link[:, : columns.size]


def part_products(ref, origins, schur_ref, products):
    side_count, share = ref.shape[2:]
    for place, origin in enumerate(origins):
        rows = pl.ds(pl.multiple_of(origin * share, share), share)
        field = ref[place].reshape(2 * side_count, share)
        terms = real_products(field, schur_ref.at[:, rows, :])
        products = terms if products is None else [a + b for a, b in zip(products, terms)]
    return products


def products_kernel(turn, sources, which, *refs):
    schur_ref, products_ref = refs[len(which)], refs[-1]

    @gated(turn)
    def _():
        origins = sources(lax.axis_index("xy"))
        products = None
        if len(refs) > len(which) + 2:
            products = [refs[len(which) + 1][part] for part in range(2)]
        for ref, (part, core) in zip(refs, which):
            products = part_products(ref, origins[part][core], schur_ref, products)
        for part in range(2):
            products_ref[part] = products[part]


def late_kernel(turn, sources, names, *refs):
    named = dict(zip(names, refs))
    kept_ref, message_ref = refs[-2:]

    @gated(turn)
    def _():
        origins = sources(lax.axis_index("xy"))[-1][1]
        products = [named["products"][part] for part in range(2)]
        products = part_products(named["other"], origins, named["schur"], products)
        for part, value in enumerate(combined(products)):
            value = named["mask"][...] * value
            if "kept" in named:
                value = named["kept"][part] + value
            kept_ref[part] = value
            if "scale" in named:
                value = named["scale"][...] * value
            if "addend" in named:
                value = named["addend"][part] + value
            message_ref[part] = value.astype(jnp.bfloat16)


def cost_of(mine):
    _, _, side_count, share = mine.shape
    return {
        "flops": 8 * side_count * share * share * mine.shape[0],
        "moved": 4 * share * share * mine.shape[0],
    }


def products_of(turn, sources, which, parts, schur, products=None):
    side_count, share = parts[0].shape[2:]
    operands = [*parts, schur] + ([] if products is None else [products])
    return in_kernel(
        functools.partial(products_kernel, turn, sources, which),
        [((2, 2 * side_count, share), jnp.float32)],
        [resident(value) for value in operands],
        **cost_of(parts[0]),
    )[0]


def first_products(turn, sources, schur, mine):
    return products_of(turn, sources, [(0, 0)], [mine], schur)


def more_products(turn, sources, pieces, schur, products):
    (_, other), (more, _) = pieces
    return products_of(turn, sources, [(0, 1), (1, 0)], [other, more], schur, products)


def sweep_step(turn, sources, pieces, schur, products, kept, message, adds, **others):
    products = more_products(turn, sources, pieces, schur, products)
    named = {"products": products, "other": pieces[-1][1], "schur": schur}
    named.update({name: value for name, value in others.items() if value is not None})
    named["kept" if adds else "old"], named["message"] = kept, message
    count = len(named)
    return in_kernel(
        functools.partial(late_kernel, turn, sources, list(named)),
        [(kept.shape, kept.dtype), (message.shape, message.dtype)],
        [resident(value) for value in named.values()],
        aliases={count - 2: 0, count - 1: 1},
        **cost_of(pieces[-1][1]),
    )


def last_step(turn, sources, pieces, schur, products, mask, kepts):
    products = more_products(turn, sources, pieces, schur, products)
    operands = [products, pieces[-1][1], schur, mask] + kepts
    return in_kernel(
        functools.partial(last_kernel, turn, sources),
        [
            (kepts[0].shape, kepts[0].dtype),
            ((len(kepts),) + kepts[0].shape, jnp.bfloat16),
        ],
        [resident(value) for value in operands],
        aliases={4: 0},
        **cost_of(pieces[-1][1]),
    )


def last_kernel(turn, sources, products_ref, other_ref, schur_ref, mask_ref, *refs):
    kepts, kept_ref, message_ref = refs[:-2], refs[-2], refs[-1]
    for panel in range(1, len(kepts)):
        message_ref[panel] = kepts[panel][...].astype(jnp.bfloat16)

    @gated(turn)
    def _():
        origins = sources(lax.axis_index("xy"))[-1][1]
        products = [products_ref[part] for part in range(2)]
        products = part_products(other_ref, origins, schur_ref, products)
        for part, value in enumerate(combined(products)):
            value = kepts[0][part] + mask_ref[...] * value
            kept_ref[part] = value
            message_ref[0, part] = value.astype(jnp.bfloat16)

    @pl.when(lax.axis_index("gz") != turn)
    def _():
        message_ref[0] = kepts[0][...].astype(jnp.bfloat16)


def pick_kernel(sources, which, *refs):
    rows_ref, picked_ref = refs[len(which)], refs[-1]
    origins = sources(lax.axis_index("xy"))
    picked = None
    if len(refs) > len(which) + 2:
        picked = [refs[len(which) + 1][panel] for panel in range(picked_ref.shape[0])]
    for ref, (part, core) in zip(refs, which):
        picked = picks(ref, rows_ref, origins[part][core], picked)
    for panel, value in enumerate(picked):
        picked_ref[panel] = value


def picks(ref, rows_ref, origins, picked):
    _, panel_count, _, side_count, share = ref.shape
    bound = rows_ref.shape[1]
    found = []
    for panel in range(panel_count):
        total = picked[panel] if picked else jnp.zeros((2 * side_count, bound), jnp.float32)
        for place, origin in enumerate(origins):
            rows = origin * share + lax.broadcasted_iota(jnp.int32, (share, bound), 0)
            chosen = jnp.where(rows == rows_ref[pl.ds(panel, 1), :], 1.0, 0.0).astype(jnp.bfloat16)
            field = ref[place, panel].reshape(2 * side_count, share)
            total += jnp.dot(field, chosen, preferred_element_type=jnp.float32)
        found.append(total)
    return found


def first_pick_kernel(sources, mine_ref, rows_ref, *refs):
    kepts, (picked_ref, chosen_ref, fronts_ref, sems) = refs[:-4], refs[-4:]
    copies = [
        pltpu.make_async_copy(kept_ref, fronts_ref.at[panel], sems.at[panel])
        for panel, kept_ref in enumerate(kepts)
    ]
    for copy in copies:
        copy.start()
    (origins, _), (_, lasts) = sources(lax.axis_index("xy"))
    for panel, value in enumerate(picks(mine_ref, rows_ref, origins, None)):
        picked_ref[panel] = value
    panel_count, _, share, bound = chosen_ref.shape
    for panel in range(panel_count):
        for index, origin in enumerate(lasts):
            rows = origin * share + lax.broadcasted_iota(jnp.int32, (share, bound), 0)
            hits = jnp.where(rows == rows_ref[pl.ds(panel, 1), :], 1.0, 0.0)
            chosen_ref[panel, index] = hits.astype(jnp.bfloat16)
    for copy in copies:
        copy.wait()


def inner_kernel(
    picked_ref, last_ref, chosen_ref, coupling_ref, inverse_ref, solved_ref, out_ref, inner_ref, sems
):
    contract = (((1,), (1,)), ((), ()))
    _, panel_count, _, side_count, share = last_ref.shape
    picked = []
    for panel in range(panel_count):
        total = picked_ref[panel]
        for place in range(last_ref.shape[0]):
            field = last_ref[place, panel].reshape(2 * side_count, share)
            total += jnp.dot(field, chosen_ref[panel, place], preferred_element_type=jnp.float32)
        picked.append(total)
    lifted = [
        combined(
            [
                lax.dot_general(
                    value.astype(jnp.bfloat16),
                    coupling_ref[panel, 0, part],
                    contract,
                    preferred_element_type=jnp.float32,
                )
                for part in range(2)
            ]
        )
        for panel, value in enumerate(picked)
    ]
    copies = []
    for panel, value in enumerate(lifted):
        field = jnp.concatenate(value).astype(jnp.bfloat16)
        back = combined(real_products(field, inverse_ref.at[panel, 0]))
        for part in range(2):
            inner_ref[panel, part] = solved_ref[panel, part] - back[part]
        copies.append(
            pltpu.make_async_copy(inner_ref.at[panel], out_ref.at[panel], sems.at[panel])
        )
        copies[-1].start()
    for copy in copies:
        copy.wait()


def on_device(
    source_inner, source_front, inner_inverse, coupling, schur_inverse, front_rows, link, front_size
):
    peers, groups = lax.axis_size("xy"), lax.axis_size("gz")
    panel_count, _, side_count, share = source_front.shape
    bound = front_rows.shape[1]
    local = source_inner.shape[3]

    tail_rows = 2 * panel_count + 2 * -(-share // bound)
    tail_rows += -tail_rows % 16
    sent_rows = 2 * side_count * panel_count + tail_rows
    taken = [source_inner, inner_inverse, coupling, front_rows, link, source_front]
    row = ((1, share), jnp.float32)
    arriving = ((peers // 4, 1, 1, share), jnp.float32)
    solved, sent, _, inverse_held, coupling_held, rows_held, _, source_held, *scales = in_kernel(
        local_kernel,
        [
            ((panel_count, 2, side_count, local), jnp.float32),
            ((sent_rows, bound), jnp.bfloat16),
        ]
        + [(value.shape, value.dtype) for value in taken]
        + [row] * (3 * panel_count)
        + [arriving] * 4,
        [in_hbm(value) for value in taken + [front_size]],
        specs=[IN_HBM] * (len(taken) + 1),
        scratch=[
            pltpu.SMEM(front_size.shape, jnp.int32),
            pltpu.VMEM((tail_rows, bound), jnp.float32),
            pltpu.SemaphoreType.DMA((5 * panel_count + 4,)),
        ],
    )
    masks, forward_scales = scales[:panel_count], scales[panel_count : 2 * panel_count]
    backward_scales, met = scales[2 * panel_count : 3 * panel_count], scales[3 * panel_count :]

    def push(panel, shards, contrib=None):
        operands = shards + ([] if contrib is None else [contrib])
        return in_kernel(
            functools.partial(push_kernel, panel, panel_count, len(shards)),
            [((2 * side_count, share), jnp.float32)],
            [resident(value) for value in operands],
        )[0]

    shards, contrib, schurs = gathered_within(
        sent, None, lambda mine: push(0, [mine]), [loaded(schur_inverse, sent)]
    )
    shards = [shard for part in shards for shard in part]
    contrib = push(0, shards[1:3], contrib)
    operands = [masks[0], contrib, source_held, shards[3]]
    base, message = in_kernel(
        functools.partial(base_kernel, 0, panel_count),
        [((2, side_count, share), jnp.float32), ((2, side_count, share), jnp.bfloat16)],
        [resident(value) for value in operands],
        moved=2**22,
    )
    bases = [base]
    for panel in range(1, panel_count):
        operands = [resident(value) for value in (masks[panel], source_held, *shards)]
        base, schur = in_kernel(
            functools.partial(later_kernel, panel, panel_count),
            [((2, side_count, share), jnp.float32), (schur_inverse.shape[1:], schur_inverse.dtype)],
            operands + [in_hbm(schur_inverse), message],
            specs=[IN_VMEM] * len(operands) + [IN_HBM, pl.BlockSpec(memory_space=pl.ANY)],
            scratch=[pltpu.SemaphoreType.DMA((8,))],
            moved=2**23,
        )
        bases.append(base)
        schurs.append(schur)
    met[:2] = in_kernel(
        functools.partial(link_kernel, panel_count, side_count),
        [arriving] * 2,
        [resident(value) for value in (met[0], met[1], shards[0], shards[2])],
    )

    kept = [jnp.zeros((2, side_count, share), jnp.float32) for _ in range(panel_count)]
    within, across = sources_by(masks_within(peers)), sources_by(masks_across(peers))
    order = [(turn, panel) for turn in range(groups) for panel in range(panel_count)]
    steps = [(None, 0, True)] + [step + (True,) for step in order[1:]]
    steps += [step + (False,) for step in reversed(order[:-1])]
    for count, (turn, panel, forward) in enumerate(steps):
        if forward and panel == 0 and turn is not None:
            low, by, scales = turn - 1, 1, met[:2]
        elif not forward and panel == panel_count - 1:
            low, by, scales = turn, -1, met[2:]
        else:
            low = None
        sources = within if low is None else across
        first = functools.partial(first_products, turn, sources, schurs[panel])
        if low is not None:
            pieces, products = crossed(message, low, by, scales, first)
        elif count == 0:
            beside = (bases[1:], schurs[1:], met)
            pieces, products, beside = gathered_within(message, None, first, beside)
            bases[1:], schurs[1:], met = beside
        else:
            pieces, products, _ = gathered_within(message, turn, first)
        scale = addend = None
        if forward and panel < panel_count - 1:
            scale, addend = forward_scales[panel + 1], bases[panel + 1]
        elif not forward or turn == groups - 1:
            scale = backward_scales[panel]
        if count == len(steps) - 1:
            kept[0], message = last_step(turn, sources, pieces, schurs[0], products, masks[0], kept)
        else:
            kept[panel], message = sweep_step(
                turn, sources, pieces, schurs[panel], products, kept[panel], message,
                not forward or (panel == 0 and turn is not None),
                mask=masks[panel], scale=scale, addend=addend,
            )


    def pick(which, parts, *picked):
        return in_kernel(
            functools.partial(pick_kernel, within, which),
            [((panel_count, 2 * side_count, bound), jnp.float32)],
            [resident(value) for value in (*parts, rows_held, *picked)],
            moved=2**22,
        )[0]

    def first_pick(mine):
        last_count = peers // 2 - mine.shape[0]
        operands = [mine, rows_held, *kept]
        return pl.pallas_call(
            functools.partial(first_pick_kernel, within),
            out_shape=(
                pltpu.VMEM((panel_count, 2 * side_count, bound), jnp.float32),
                pltpu.VMEM((panel_count, last_count, share, bound), jnp.bfloat16),
                jax.ShapeDtypeStruct((panel_count, 2, side_count, share), jnp.float32),
            ),
            in_specs=[IN_VMEM] * len(operands),
            out_specs=(IN_VMEM, IN_VMEM, IN_HBM),
            scratch_shapes=[pltpu.SemaphoreType.DMA((panel_count,))],
            compiler_params=pltpu.CompilerParams(vmem_limit_bytes=16 * 2**20),
            cost_estimate=pl.CostEstimate(flops=0, bytes_accessed=2**22, transcendentals=0),
        )(*[resident(value) for value in operands])

    pieces, (picked, chosen, fronts), _ = gathered_within(message, None, first_pick)
    (_, other), (more, last) = pieces
    picked = pick([(0, 1), (1, 0)], [other, more], picked)
    operands = [picked, last, chosen, coupling_held, inverse_held, solved]
    inner = pl.pallas_call(
        inner_kernel,
        out_shape=jax.ShapeDtypeStruct(solved.shape, jnp.float32),
        in_specs=[IN_VMEM] * len(operands),
        out_specs=IN_HBM,
        scratch_shapes=[
            pltpu.VMEM(solved.shape, jnp.float32),
            pltpu.SemaphoreType.DMA((panel_count,)),
        ],
        compiler_params=pltpu.CompilerParams(vmem_limit_bytes=16 * 2**20),
    )(*[resident(value) for value in operands])
    return inner, fronts


def solution(mesh):
    placed = (
        P("gz", None, None, "xy"),
        P("gz", None, None, "xy"),
        P("gz", "xy", None, None, None),
        P("gz", "xy", None, None, None),
        P("gz", None, None, "xy"),
        P("gz", "xy"),
        P("gz", "xy"),
        P("gz"),
    )
    return jax.shard_map(
        on_device,
        mesh=mesh,
        in_specs=placed,
        out_specs=(P("gz", None, None, "xy"), P("gz", None, None, "xy")),
        check_vma=False,
    )
```

```python
import functools

import jax
import jax.numpy as jnp
from jax import lax
from jax.experimental import pallas as pl
from jax.experimental.pallas import tpu as pltpu
from jax.sharding import PartitionSpec as P

IN_VMEM = pl.BlockSpec(memory_space=pltpu.VMEM)


IN_HBM = pl.BlockSpec(memory_space=pltpu.HBM)
IN_SMEM = pl.BlockSpec(memory_space=pltpu.SMEM)


def resident(array):
    return pltpu.with_memory_space_constraint(array, pltpu.VMEM)


def in_hbm(array):
    return pltpu.with_memory_space_constraint(array, pltpu.HBM)


def swapped(shard, mask, turn=None):
    peers, groups = lax.axis_size("xy"), lax.axis_size("gz")
    pairs = []
    for group in range(groups):
        used = mask if turn is None or group == turn else 1
        pairs += [(group * peers + peer, group * peers + (peer ^ used)) for peer in range(peers)]
    return lax.ppermute(shard, ("gz", "xy"), pairs)


def masks_within(peers):
    masks = [0] + list(reversed(range(2, peers, 2)))
    return masks[: peers // 4], masks[peers // 4 :]


def in_parts(one, fetched, first, beside=(), join=jnp.stack):
    pieces = [(one, swapped(one, 1))]
    made = first(one)
    fetched, made, beside = lax.optimization_barrier((fetched, made, beside))
    two = join(fetched)
    pieces.append((two, swapped(two, 1)))
    return pieces, made, beside


def gathered_within(message, turn, first, beside=()):
    one, two = [
        [swapped(message, mask, turn) if mask else message for mask in part]
        for part in masks_within(lax.axis_size("xy"))
    ]
    return in_parts(jnp.stack(one), two, first, beside)


def sources_by(parts):
    def sources(me):
        found = []
        for masks in parts:
            mine = [me ^ mask for mask in masks]
            found.append((mine, [peer ^ 1 for peer in mine]))
        return found

    return sources


def masks_across(peers):
    masks = list(reversed(range(0, peers, 2)))
    return masks[: peers // 4], masks[peers // 4 :]


def crossed(message, low, by, scales, first):
    peers, groups = lax.axis_size("xy"), lax.axis_size("gz")

    def across(mask):
        pairs = []
        for group in range(groups):
            lower = group if (group - low) % 2 == 0 else group - 1
            joined = 0 <= lower and lower + 1 < groups
            for peer in range(peers):
                if mask == 0:
                    place = (2 * lower + 1 - group) * peers + peer if joined else group * peers + (peer ^ 1)
                elif joined and group == (lower if by > 0 else lower + 1):
                    place = (group + by) * peers + (peer ^ mask)
                else:
                    continue
                pairs.append((group * peers + peer, place))
        return lax.ppermute(message, ("gz", "xy"), pairs)

    def scaled(part, scale):
        return (scale * jnp.stack(part).astype(jnp.float32)).astype(jnp.bfloat16)

    one, two = [[across(mask) for mask in part] for part in masks_across(peers)]
    join = functools.partial(scaled, scale=scales[1])
    return in_parts(scaled(one, scales[0]), two, first, join=join)[:2]


def gated(turn):
    def wrap(body):
        if turn is None:
            body()
        else:
            pl.when(lax.axis_index("gz") == turn)(body)

    return wrap


def in_kernel(body, outs, operands, aliases=None, specs=None, scratch=(), flops=0, moved=0):
    return pl.pallas_call(
        body,
        out_shape=tuple(pltpu.VMEM(shape, dtype) for shape, dtype in outs),
        in_specs=specs or [IN_VMEM] * len(operands),
        out_specs=(IN_VMEM,) * len(outs),
        scratch_shapes=scratch,
        input_output_aliases=aliases or {},
        compiler_params=pltpu.CompilerParams(vmem_limit_bytes=16 * 2**20),
        cost_estimate=pl.CostEstimate(flops=flops, bytes_accessed=moved, transcendentals=0),
    )(*operands)


def real_products(field, matrix):
    return [
        jnp.dot(field, matrix[part], preferred_element_type=jnp.float32) for part in range(2)
    ]


def combined(products):
    first, second = products
    count = first.shape[0] // 2
    return first[:count] - second[count:], second[:count] + first[count:]


def panel_copies(panel, schur_ref, out_ref, sems):
    chunks = sems.shape[0] // 2
    rows = schur_ref.shape[2] // chunks
    copies = []
    for part in range(2):
        for chunk in range(chunks):
            span = pl.ds(chunk * rows, rows)
            copies.append(
                pltpu.make_async_copy(
                    schur_ref.at[panel, part, span, :],
                    out_ref.at[part, span, :],
                    sems.at[part * chunks + chunk],
                )
            )
    for copy in copies:
        copy.start()
    return copies


def load_kernel(schur_ref, after_ref, out_ref, sems):
    del after_ref
    for copy in panel_copies(0, schur_ref, out_ref, sems):
        copy.wait()


def loaded(schur, after):
    return in_kernel(
        load_kernel,
        [(schur.shape[1:], schur.dtype)],
        [in_hbm(schur), after],
        specs=[IN_HBM, pl.BlockSpec(memory_space=pl.ANY)],
        scratch=[pltpu.SemaphoreType.DMA((8,))],
        moved=schur.dtype.itemsize * schur[0].size,
    )[0]


def local_kernel(*refs):
    operands, size_in, (solved_ref, sent_ref), held = refs[:6], refs[6], refs[7:9], refs[9:15]
    rows_out, met, (sizes, tail_ref, sems) = refs[15:-7], refs[-7:-3], refs[-3:]
    source_ref, inverse_ref, coupling_ref, rows_ref, link_ref, _ = held
    panel_count, _, side_count, _ = source_ref.shape
    bound, share = sent_ref.shape[1], link_ref.shape[1]
    ends = []
    for panel in range(panel_count):
        ends.append((operands[0].at[panel], held[0].at[panel]))
        for operand, place in zip(operands[1:3], held[1:3]):
            for part in range(2):
                ends.append((operand.at[panel, 0, part], place.at[panel, 0, part]))
    ends += list(zip(operands[3:], held[3:])) + [(size_in, sizes)]
    copies = [
        pltpu.make_async_copy(operand, place, sems.at[index])
        for index, (operand, place) in enumerate(ends)
    ]
    for copy in copies:
        copy.start()
    for panel in range(panel_count):
        for copy in copies[5 * panel : 5 * panel + 3]:
            copy.wait()
        field = source_ref[panel].astype(jnp.bfloat16).reshape(2 * side_count, -1)
        solved = combined(real_products(field, inverse_ref.at[panel, 0]))
        for part in range(2):
            solved_ref[panel, part] = solved[part]
        field = jnp.concatenate(solved).astype(jnp.bfloat16)
        for copy in copies[5 * panel + 3 : 5 * panel + 5]:
            copy.wait()
        pushed = combined(real_products(field, coupling_ref.at[panel, 0]))
        for part in range(2):
            start = (2 * panel + part) * side_count
            sent_ref[pl.ds(start, side_count), :] = pushed[part].astype(jnp.bfloat16)
    for copy in copies[5 * panel_count :]:
        copy.wait()
    tail_ref[...] = jnp.zeros(tail_ref.shape, jnp.float32)
    for panel in range(panel_count):
        rows = rows_ref[pl.ds(panel, 1), :]
        tail_ref[pl.ds(panel, 1), :] = (rows >> 8).astype(jnp.float32)
        tail_ref[pl.ds(panel_count + panel, 1), :] = (rows & 255).astype(jnp.float32)
    row = 2 * panel_count
    for start in range(0, share, bound):
        width = min(bound, share - start)
        link = link_ref[pl.ds(0, 1), pl.ds(start, width)]
        high = link.astype(jnp.bfloat16).astype(jnp.float32)
        tail_ref[pl.ds(row, 1), pl.ds(0, width)] = high
        tail_ref[pl.ds(row + 1, 1), pl.ds(0, width)] = link - high
        row += 2
    first = 2 * side_count * panel_count
    sent_ref[pl.ds(first, tail_ref.shape[0]), :] = tail_ref[...].astype(jnp.bfloat16)
    me = lax.axis_index("xy")
    masks = [live(sizes, panel, me * share, share) for panel in range(panel_count)]
    for panel in range(panel_count):
        link = link_ref[pl.ds(panel, 1), :]
        rows_out[panel][...] = masks[panel]
        rows_out[panel_count + panel][...] = masks[panel] * link
        rows_out[2 * panel_count + panel][...] = link * masks[panel - 1] if panel else link
    for half, part in enumerate(masks_across(4 * met[0].shape[0])):
        for index, mask in enumerate(part):
            start = (me ^ mask) * share
            met[half][index, 0] = live(sizes, 0, start, share)
            met[2 + half][index, 0] = live(sizes, panel_count - 1, start, share)


def tail_of(ref, place, first):
    return ref[place, pl.ds(first, ref.shape[1] - first), :].astype(jnp.float32)


def live(size_ref, panel, start, share):
    rows = start + lax.broadcasted_iota(jnp.int32, (1, share), 1)
    return jnp.where(rows < size_ref[panel], 1.0, 0.0)


def pushed_up(panel, panel_count, count, share, refs, contrib):
    bound = refs[0].shape[2]
    own_rows = lax.axis_index("xy") * share + lax.broadcasted_iota(jnp.int32, (share, bound), 0)
    contract = (((1,), (1,)), ((), ()))
    for ref in refs:
        for place in range(ref.shape[0]):
            values = ref[place, pl.ds(count * panel, count), :]
            tail = tail_of(ref, place, count * panel_count)
            high = tail[panel : panel + 1]
            low = tail[panel_count + panel : panel_count + panel + 1]
            places = (256.0 * high + low).astype(jnp.int32)
            hits = jnp.where(own_rows == places, 1.0, 0.0).astype(jnp.bfloat16)
            contrib += lax.dot_general(values, hits, contract, preferred_element_type=jnp.float32)
    return contrib


def push_kernel(panel, panel_count, parts, *refs):
    contrib_ref = refs[-1]
    count, share = contrib_ref.shape
    contrib = refs[parts][...] if len(refs) > parts + 1 else jnp.zeros((count, share), jnp.float32)
    contrib_ref[...] = pushed_up(panel, panel_count, count, share, refs[:parts], contrib)


def base_kernel(panel, panel_count, mask_ref, contrib_ref, source_ref, *refs):
    refs, base_ref, message_ref = refs[:-2], refs[-2], refs[-1]
    _, side_count, share = base_ref.shape
    count = 2 * side_count
    contrib = pushed_up(panel, panel_count, count, share, refs, contrib_ref[...])
    for part in range(2):
        rows = slice(part * side_count, (part + 1) * side_count)
        base = mask_ref[...] * (source_ref[panel, part] - contrib[rows])
        base_ref[part] = base
        message_ref[part] = base.astype(jnp.bfloat16)


def later_kernel(panel, panel_count, mask_ref, source_ref, *refs):
    shards, schur_ref, base_ref, out_ref, sems = refs[:4], refs[4], refs[6], refs[7], refs[8]
    copies = panel_copies(panel, schur_ref, out_ref, sems)
    _, side_count, share = base_ref.shape
    count = 2 * side_count
    zeros = jnp.zeros((count, share), jnp.float32)
    contrib = pushed_up(panel, panel_count, count, share, shards, zeros)
    for part in range(2):
        rows = slice(part * side_count, (part + 1) * side_count)
        base_ref[part] = mask_ref[...] * (source_ref[panel, part] - contrib[rows])
    for copy in copies:
        copy.wait()


def link_kernel(panel_count, side_count, one_mask, two_mask, one_ref, two_ref, one_out, two_out):
    share, bound = one_out.shape[3], one_ref.shape[2]
    peers = 4 * one_out.shape[0]
    tails = {}
    for ref, part in zip((one_ref, two_ref), masks_within(peers)):
        for index, mask in enumerate(part):
            tails[mask] = tail_of(ref, index, 2 * side_count * panel_count)
    for mask_ref, out, part in zip((one_mask, two_mask), (one_out, two_out), masks_across(peers)):
        for index, mask in enumerate(part):
            for piece, place in enumerate(range(0, share, bound)):
                columns = pl.ds(place, min(bound, share - place))
                row = 2 * (panel_count + piece)
                link = tails[mask][row : row + 1] + tails[mask][row + 1 : row + 2]
                out[index, 0, :, columns] = mask_ref[index, 0, :, columns] * link[:, : columns.size]


def part_products(ref, origins, schur_ref, products):
    side_count, share = ref.shape[2:]
    for place, origin in enumerate(origins):
        rows = pl.ds(pl.multiple_of(origin * share, share), share)
        field = ref[place].reshape(2 * side_count, share)
        terms = real_products(field, schur_ref.at[:, rows, :])
        products = terms if products is None else [a + b for a, b in zip(products, terms)]
    return products


def products_kernel(turn, sources, which, *refs):
    schur_ref, products_ref = refs[len(which)], refs[-1]

    @gated(turn)
    def _():
        origins = sources(lax.axis_index("xy"))
        products = None
        if len(refs) > len(which) + 2:
            products = [refs[len(which) + 1][part] for part in range(2)]
        for ref, (part, core) in zip(refs, which):
            products = part_products(ref, origins[part][core], schur_ref, products)
        for part in range(2):
            products_ref[part] = products[part]


def late_kernel(turn, sources, names, *refs):
    named = dict(zip(names, refs))
    kept_ref, message_ref = refs[-2:]

    @gated(turn)
    def _():
        origins = sources(lax.axis_index("xy"))[-1][1]
        products = [named["products"][part] for part in range(2)]
        products = part_products(named["other"], origins, named["schur"], products)
        for part, value in enumerate(combined(products)):
            value = named["mask"][...] * value
            if "kept" in named:
                value = named["kept"][part] + value
            kept_ref[part] = value
            if "scale" in named:
                value = named["scale"][...] * value
            if "addend" in named:
                value = named["addend"][part] + value
            message_ref[part] = value.astype(jnp.bfloat16)


def cost_of(mine):
    _, _, side_count, share = mine.shape
    return {
        "flops": 8 * side_count * share * share * mine.shape[0],
        "moved": 4 * share * share * mine.shape[0],
    }


def products_of(turn, sources, which, parts, schur, products=None):
    side_count, share = parts[0].shape[2:]
    operands = [*parts, schur] + ([] if products is None else [products])
    return in_kernel(
        functools.partial(products_kernel, turn, sources, which),
        [((2, 2 * side_count, share), jnp.float32)],
        [resident(value) for value in operands],
        **cost_of(parts[0]),
    )[0]


def first_products(turn, sources, schur, mine):
    return products_of(turn, sources, [(0, 0)], [mine], schur)


def more_products(turn, sources, pieces, schur, products):
    (_, other), (more, _) = pieces
    return products_of(turn, sources, [(0, 1), (1, 0)], [other, more], schur, products)


def sweep_step(turn, sources, pieces, schur, products, kept, message, adds, **others):
    products = more_products(turn, sources, pieces, schur, products)
    named = {"products": products, "other": pieces[-1][1], "schur": schur}
    named.update({name: value for name, value in others.items() if value is not None})
    named["kept" if adds else "old"], named["message"] = kept, message
    count = len(named)
    return in_kernel(
        functools.partial(late_kernel, turn, sources, list(named)),
        [(kept.shape, kept.dtype), (message.shape, message.dtype)],
        [resident(value) for value in named.values()],
        aliases={count - 2: 0, count - 1: 1},
        **cost_of(pieces[-1][1]),
    )


def last_step(turn, sources, pieces, schur, products, mask, kepts):
    products = more_products(turn, sources, pieces, schur, products)
    operands = [products, pieces[-1][1], schur, mask] + kepts
    return in_kernel(
        functools.partial(last_kernel, turn, sources),
        [
            (kepts[0].shape, kepts[0].dtype),
            ((len(kepts),) + kepts[0].shape, jnp.bfloat16),
        ],
        [resident(value) for value in operands],
        aliases={4: 0},
        **cost_of(pieces[-1][1]),
    )


def last_kernel(turn, sources, products_ref, other_ref, schur_ref, mask_ref, *refs):
    kepts, kept_ref, message_ref = refs[:-2], refs[-2], refs[-1]
    for panel in range(1, len(kepts)):
        message_ref[panel] = kepts[panel][...].astype(jnp.bfloat16)

    @gated(turn)
    def _():
        origins = sources(lax.axis_index("xy"))[-1][1]
        products = [products_ref[part] for part in range(2)]
        products = part_products(other_ref, origins, schur_ref, products)
        for part, value in enumerate(combined(products)):
            value = kepts[0][part] + mask_ref[...] * value
            kept_ref[part] = value
            message_ref[0, part] = value.astype(jnp.bfloat16)

    @pl.when(lax.axis_index("gz") != turn)
    def _():
        message_ref[0] = kepts[0][...].astype(jnp.bfloat16)


def pick_kernel(sources, which, *refs):
    rows_ref, picked_ref = refs[len(which)], refs[-1]
    origins = sources(lax.axis_index("xy"))
    picked = None
    if len(refs) > len(which) + 2:
        picked = [refs[len(which) + 1][panel] for panel in range(picked_ref.shape[0])]
    for ref, (part, core) in zip(refs, which):
        picked = picks(ref, rows_ref, origins[part][core], picked)
    for panel, value in enumerate(picked):
        picked_ref[panel] = value


def picks(ref, rows_ref, origins, picked):
    _, panel_count, _, side_count, share = ref.shape
    bound = rows_ref.shape[1]
    found = []
    for panel in range(panel_count):
        total = picked[panel] if picked else jnp.zeros((2 * side_count, bound), jnp.float32)
        for place, origin in enumerate(origins):
            rows = origin * share + lax.broadcasted_iota(jnp.int32, (share, bound), 0)
            chosen = jnp.where(rows == rows_ref[pl.ds(panel, 1), :], 1.0, 0.0).astype(jnp.bfloat16)
            field = ref[place, panel].reshape(2 * side_count, share)
            total += jnp.dot(field, chosen, preferred_element_type=jnp.float32)
        found.append(total)
    return found


def first_pick_kernel(sources, mine_ref, rows_ref, picked_ref, chosen_ref):
    (origins, _), (_, lasts) = sources(lax.axis_index("xy"))
    for panel, value in enumerate(picks(mine_ref, rows_ref, origins, None)):
        picked_ref[panel] = value
    panel_count, _, share, bound = chosen_ref.shape
    for panel in range(panel_count):
        for index, origin in enumerate(lasts):
            rows = origin * share + lax.broadcasted_iota(jnp.int32, (share, bound), 0)
            hits = jnp.where(rows == rows_ref[pl.ds(panel, 1), :], 1.0, 0.0)
            chosen_ref[panel, index] = hits.astype(jnp.bfloat16)


def inner_kernel(
    picked_ref, last_ref, chosen_ref, coupling_ref, inverse_ref, solved_ref, out_ref, inner_ref, sems
):
    contract = (((1,), (1,)), ((), ()))
    _, panel_count, _, side_count, share = last_ref.shape
    picked = []
    for panel in range(panel_count):
        total = picked_ref[panel]
        for place in range(last_ref.shape[0]):
            field = last_ref[place, panel].reshape(2 * side_count, share)
            total += jnp.dot(field, chosen_ref[panel, place], preferred_element_type=jnp.float32)
        picked.append(total)
    lifted = [
        combined(
            [
                lax.dot_general(
                    value.astype(jnp.bfloat16),
                    coupling_ref[panel, 0, part],
                    contract,
                    preferred_element_type=jnp.float32,
                )
                for part in range(2)
            ]
        )
        for panel, value in enumerate(picked)
    ]
    copies = []
    for panel, value in enumerate(lifted):
        field = jnp.concatenate(value).astype(jnp.bfloat16)
        back = combined(real_products(field, inverse_ref.at[panel, 0]))
        for part in range(2):
            inner_ref[panel, part] = solved_ref[panel, part] - back[part]
        copies.append(
            pltpu.make_async_copy(inner_ref.at[panel], out_ref.at[panel], sems.at[panel])
        )
        copies[-1].start()
    for copy in copies:
        copy.wait()


def on_device(
    source_inner, source_front, inner_inverse, coupling, schur_inverse, front_rows, link, front_size
):
    peers, groups = lax.axis_size("xy"), lax.axis_size("gz")
    panel_count, _, side_count, share = source_front.shape
    bound = front_rows.shape[1]
    local = source_inner.shape[3]

    tail_rows = 2 * panel_count + 2 * -(-share // bound)
    tail_rows += -tail_rows % 16
    sent_rows = 2 * side_count * panel_count + tail_rows
    taken = [source_inner, inner_inverse, coupling, front_rows, link, source_front]
    row = ((1, share), jnp.float32)
    arriving = ((peers // 4, 1, 1, share), jnp.float32)
    solved, sent, _, inverse_held, coupling_held, rows_held, _, source_held, *scales = in_kernel(
        local_kernel,
        [
            ((panel_count, 2, side_count, local), jnp.float32),
            ((sent_rows, bound), jnp.bfloat16),
        ]
        + [(value.shape, value.dtype) for value in taken]
        + [row] * (3 * panel_count)
        + [arriving] * 4,
        [in_hbm(value) for value in taken + [front_size]],
        specs=[IN_HBM] * (len(taken) + 1),
        scratch=[
            pltpu.SMEM(front_size.shape, jnp.int32),
            pltpu.VMEM((tail_rows, bound), jnp.float32),
            pltpu.SemaphoreType.DMA((5 * panel_count + 4,)),
        ],
    )
    masks, forward_scales = scales[:panel_count], scales[panel_count : 2 * panel_count]
    backward_scales, met = scales[2 * panel_count : 3 * panel_count], scales[3 * panel_count :]

    def push(panel, shards, contrib=None):
        operands = shards + ([] if contrib is None else [contrib])
        return in_kernel(
            functools.partial(push_kernel, panel, panel_count, len(shards)),
            [((2 * side_count, share), jnp.float32)],
            [resident(value) for value in operands],
        )[0]

    shards, contrib, schurs = gathered_within(
        sent, None, lambda mine: push(0, [mine]), [loaded(schur_inverse, sent)]
    )
    shards = [shard for part in shards for shard in part]
    contrib = push(0, shards[1:3], contrib)
    operands = [masks[0], contrib, source_held, shards[3]]
    base, message = in_kernel(
        functools.partial(base_kernel, 0, panel_count),
        [((2, side_count, share), jnp.float32), ((2, side_count, share), jnp.bfloat16)],
        [resident(value) for value in operands],
        moved=2**22,
    )
    bases = [base]
    for panel in range(1, panel_count):
        operands = [resident(value) for value in (masks[panel], source_held, *shards)]
        base, schur = in_kernel(
            functools.partial(later_kernel, panel, panel_count),
            [((2, side_count, share), jnp.float32), (schur_inverse.shape[1:], schur_inverse.dtype)],
            operands + [in_hbm(schur_inverse), message],
            specs=[IN_VMEM] * len(operands) + [IN_HBM, pl.BlockSpec(memory_space=pl.ANY)],
            scratch=[pltpu.SemaphoreType.DMA((8,))],
            moved=2**23,
        )
        bases.append(base)
        schurs.append(schur)
    met[:2] = in_kernel(
        functools.partial(link_kernel, panel_count, side_count),
        [arriving] * 2,
        [resident(value) for value in (met[0], met[1], shards[0], shards[2])],
    )

    kept = [jnp.zeros((2, side_count, share), jnp.float32) for _ in range(panel_count)]
    within, across = sources_by(masks_within(peers)), sources_by(masks_across(peers))
    order = [(turn, panel) for turn in range(groups) for panel in range(panel_count)]
    steps = [(None, 0, True)] + [step + (True,) for step in order[1:]]
    steps += [step + (False,) for step in reversed(order[:-1])]
    for count, (turn, panel, forward) in enumerate(steps):
        if forward and panel == 0 and turn is not None:
            low, by, scales = turn - 1, 1, met[:2]
        elif not forward and panel == panel_count - 1:
            low, by, scales = turn, -1, met[2:]
        else:
            low = None
        sources = within if low is None else across
        first = functools.partial(first_products, turn, sources, schurs[panel])
        if low is not None:
            pieces, products = crossed(message, low, by, scales, first)
        elif count == 0:
            beside = (bases[1:], schurs[1:], met)
            pieces, products, beside = gathered_within(message, None, first, beside)
            bases[1:], schurs[1:], met = beside
        else:
            pieces, products, _ = gathered_within(message, turn, first)
        scale = addend = None
        if forward and panel < panel_count - 1:
            scale, addend = forward_scales[panel + 1], bases[panel + 1]
        elif not forward or turn == groups - 1:
            scale = backward_scales[panel]
        if count == len(steps) - 1:
            kept[0], message = last_step(turn, sources, pieces, schurs[0], products, masks[0], kept)
        else:
            kept[panel], message = sweep_step(
                turn, sources, pieces, schurs[panel], products, kept[panel], message,
                not forward or (panel == 0 and turn is not None),
                mask=masks[panel], scale=scale, addend=addend,
            )

    fronts = jnp.stack(kept)

    def pick(which, parts, *picked):
        return in_kernel(
            functools.partial(pick_kernel, within, which),
            [((panel_count, 2 * side_count, bound), jnp.float32)],
            [resident(value) for value in (*parts, rows_held, *picked)],
            moved=2**22,
        )[0]

    def first_pick(mine):
        return in_kernel(
            functools.partial(first_pick_kernel, within),
            [
                ((panel_count, 2 * side_count, bound), jnp.float32),
                ((panel_count, peers // 2 - mine.shape[0], share, bound), jnp.bfloat16),
            ],
            [resident(mine), resident(rows_held)],
            moved=2**22,
        )

    pieces, (picked, chosen), _ = gathered_within(message, None, first_pick)
    (_, other), (more, last) = pieces
    picked = pick([(0, 1), (1, 0)], [other, more], picked)
    operands = [picked, last, chosen, coupling_held, inverse_held, solved]
    inner = pl.pallas_call(
        inner_kernel,
        out_shape=jax.ShapeDtypeStruct(solved.shape, jnp.float32),
        in_specs=[IN_VMEM] * len(operands),
        out_specs=IN_HBM,
        scratch_shapes=[
            pltpu.VMEM(solved.shape, jnp.float32),
            pltpu.SemaphoreType.DMA((panel_count,)),
        ],
        compiler_params=pltpu.CompilerParams(vmem_limit_bytes=16 * 2**20),
    )(*[resident(value) for value in operands])
    return inner, fronts


def solution(mesh):
    placed = (
        P("gz", None, None, "xy"),
        P("gz", None, None, "xy"),
        P("gz", "xy", None, None, None),
        P("gz", "xy", None, None, None),
        P("gz", None, None, "xy"),
        P("gz", "xy"),
        P("gz", "xy"),
        P("gz"),
    )
    return jax.shard_map(
        on_device,
        mesh=mesh,
        in_specs=placed,
        out_specs=(P("gz", None, None, "xy"), P("gz", None, None, "xy")),
        check_vma=False,
    )
```
